256 devices in a mesh: section: 8 (over z), seq: 32 (over y, x, core).
Axes of the slice: x: 4, y: 4, z: 8, core: 2. Of those that a mesh axis runs over, the one named last changes fastest.
Arguments:
- input_in_transit: bfloat16 [8, 4096, 4096], P('section', 'seq'), may hold values from -6 to 6
- mixer_norm_gain: float32 [8, 4096], P('section'), may hold values from 0.5 to 1.5
- convolution_weight: float32 [8, 4, 4096], P('section'), may hold values from -3 to 3
- convolution_bias: float32 [8, 4096], P('section'), may hold values from -2 to 2
- input_projection: bfloat16 [8, 4096, 288], P('section', 'seq'), may hold values from -0.09375 to 0.09375
- step_size_projection: bfloat16 [8, 256, 4096], P('section', None, 'seq'), may hold values from -0.375 to 0.375
- step_size_bias: float32 [8, 4096], P('section'), may hold values from -6.9 to -2.3
- log_decay_rates: float32 [8, 4096, 16], P('section'), may hold values from 0 to 2.77
- mixer_skip_weight: float32 [8, 4096], P('section'), may hold values from 0.5 to 1.5
- expert_norm_gain: float32 [8, 4096], P('section'), may hold values from 0.1 to 1.9
- router: bfloat16 [8, 4096, 16], P('section'), may hold values from -0.09375 to 0.09375
- gate_weight: bfloat16 [8, 4096, 12288], P('section', None, 'seq'), may hold values from -0.09375 to 0.09375
- up_weight: bfloat16 [8, 4096, 12288], P('section', None, 'seq'), may hold values from -0.09375 to 0.09375
- down_weight: bfloat16 [8, 12288, 4096], P('section', 'seq'), may hold values from -0.0546875 to 0.0546875
- expert_index_table: int32 [2, 8, 4096, 2], P(None, 'section', 'seq'), may hold values from 0 to 15, as said below
Outputs:
- layer_out: bfloat16 [8, 4096, 4096], P('section', 'seq')
The draws below stay inside these ranges and needn't reach their ends.
Inputs may be any that keep to these rules, and one draw needn't show every extreme that they name: `expert_index_table`: each token names two different experts of the 16; for each step and section, expert 0 is named by at most 8 tokens of any one block of 128 tokens.
All inputs are finite; a program needn't handle non-finite values.
Results may differ from the reference program's by a relative error of at most 0.0086.
Values may be sent and summed in bfloat16 or wider, within the bound.
No kernel may reach another device: no remote copies, remote signals or barrier semaphores. Data moves between devices by JAX's collectives and lax.ppermute only.
A program may use at most 128 MiB of HBM per device.

```python
import jax
import jax.numpy as jnp
from jax import lax

MODEL_DIM = 4096
NSTATE = 16
RANK = 256
KCONV = 4
FF = 12288
EXPERTS = 16
STEPS = 2
L_DEV = 128
SEQUENCE_LENGTH = 4096
CAP = 8
N_SECTION = 8
N_SEQ = 32


def draw_expert_index_table(key, part):
    block_total = STEPS * N_SECTION * (SEQUENCE_LENGTH // L_DEV)
    keys = jax.random.split(jax.random.fold_in(key, 7321), 7)
    counts = jax.random.randint(keys[0], (block_total,), CAP // 4, CAP + 1)
    full = jax.random.randint(keys[1], (block_total,), 0, 4) == 0
    forced = jax.random.randint(keys[2], (), 0, block_total)
    full = full | (jnp.arange(block_total, dtype=jnp.int32) == forced)
    counts = jnp.where(full, CAP, counts)
    scores = jax.random.randint(keys[3], (block_total, L_DEV), 0, 1 << 20) * L_DEV + jnp.arange(L_DEV, dtype=jnp.int32)[None, :]
    order = jnp.argsort(scores, axis=1, stable=True)
    ranks = jnp.argsort(order, axis=1, stable=True)
    chosen = ranks < counts[:, None]
    first = jax.random.randint(keys[4], (block_total, L_DEV), 1, EXPERTS)
    offset = jax.random.randint(keys[5], (block_total, L_DEV), 1, EXPERTS - 1)
    second = 1 + (first - 1 + offset) % (EXPERTS - 1)
    side = jax.random.randint(keys[6], (block_total, L_DEV), 0, 2)
    first = jnp.where(chosen & (side == 0), 0, first)
    second = jnp.where(chosen & (side == 1), 0, second)
    pair = jnp.stack([first, second], -1).astype(jnp.int32)
    return pair.reshape(STEPS, N_SECTION, SEQUENCE_LENGTH, 2)


def block_levels(own_key, extent, pieces, smallest, largest):
    def one(axis_at, parts):
        draws = jax.random.uniform(jax.random.fold_in(jax.random.fold_in(own_key, 6), axis_at), (parts,), jnp.float32, smallest / len(pieces), largest / len(pieces))
        return jnp.repeat(jnp.exp(draws), extent[axis_at] // parts).reshape((-1,) + (1,) * (len(extent) - axis_at - 1))

    loudness = one(*pieces[0])
    for cut in pieces[1:]:
        loudness = loudness * one(*cut)
    return loudness


def centred(rng, shape, scale, limit, pieces=(), kind=jnp.bfloat16):
    values = scale * jax.random.normal(rng, shape, jnp.float32)
    if pieces:
        values = values * block_levels(rng, shape, pieces, -0.22, 0.18)
    return jnp.clip(values, -limit, limit).astype(kind)


def setup_inputs(seed: int = 0) -> dict:
    arg_keys = jax.random.split(jax.random.key(seed), 16)
    input_in_transit = centred(arg_keys[0], (N_SECTION, SEQUENCE_LENGTH, MODEL_DIM), 1.0, 6.0, ((0, 8), (1, 32)))
    mixer_norm_gain = jnp.clip(1.0 + 0.1 * jax.random.normal(arg_keys[1], (N_SECTION, MODEL_DIM), jnp.float32), 0.5, 1.5)
    convolution_weight = centred(arg_keys[2], (N_SECTION, KCONV, MODEL_DIM), 0.5, 3.0, ((0, 8),), jnp.float32)
    convolution_bias = centred(arg_keys[3], (N_SECTION, MODEL_DIM), 0.3, 2.0, ((0, 8),), jnp.float32)
    input_projection = centred(arg_keys[4], (N_SECTION, MODEL_DIM, RANK + 2 * NSTATE), MODEL_DIM ** -0.5, 0.09375, ((0, 8), (1, 32)))
    step_size_projection = centred(arg_keys[5], (N_SECTION, RANK, MODEL_DIM), RANK ** -0.5, 0.375, ((0, 8), (2, 32)))
    step_size_bias = jnp.clip(-6.9 + 4.6000001430511475 * jax.random.uniform(arg_keys[6], (N_SECTION, MODEL_DIM), jnp.float32) ** block_levels(arg_keys[6], (N_SECTION, MODEL_DIM), ((0, 8),), -0.2, 0.2), -6.9, -2.3)
    log_decay_rates = jnp.clip(2.77 * jax.random.uniform(arg_keys[7], (N_SECTION, MODEL_DIM, NSTATE), jnp.float32) ** block_levels(arg_keys[7], (N_SECTION, MODEL_DIM, NSTATE), ((0, 8),), -0.2, 0.2), 0.0, 2.77)
    mixer_skip_weight = jnp.clip(0.5 + 1.0 * jax.random.uniform(arg_keys[8], (N_SECTION, MODEL_DIM), jnp.float32) ** block_levels(arg_keys[8], (N_SECTION, MODEL_DIM), ((0, 8),), -0.2, 0.2), 0.5, 1.5)
    expert_norm_gain = jnp.clip(1.0 + 0.18 * jax.random.normal(arg_keys[9], (N_SECTION, MODEL_DIM), jnp.float32), 0.1, 1.9)
    router = centred(arg_keys[10], (N_SECTION, MODEL_DIM, EXPERTS), MODEL_DIM ** -0.5, 0.09375, ((0, 8),))
    gate_weight = centred(arg_keys[11], (N_SECTION, MODEL_DIM, FF), MODEL_DIM ** -0.5, 0.09375, ((0, 8), (2, 32)))
    up_weight = centred(arg_keys[12], (N_SECTION, MODEL_DIM, FF), MODEL_DIM ** -0.5, 0.09375, ((0, 8), (2, 32)))
    down_weight = centred(arg_keys[13], (N_SECTION, FF, MODEL_DIM), FF ** -0.5, 0.0546875, ((0, 8), (1, 32)))
    expert_index_table = draw_expert_index_table(jax.random.fold_in(arg_keys[15], 71), 0)
    return dict(input_in_transit=input_in_transit, mixer_norm_gain=mixer_norm_gain, convolution_weight=convolution_weight, convolution_bias=convolution_bias, input_projection=input_projection, step_size_projection=step_size_projection, step_size_bias=step_size_bias, log_decay_rates=log_decay_rates, mixer_skip_weight=mixer_skip_weight, expert_norm_gain=expert_norm_gain, router=router, gate_weight=gate_weight, up_weight=up_weight, down_weight=down_weight, expert_index_table=expert_index_table)


def rms_scale(values, gain):
    as_float = values.astype(jnp.float32)
    return as_float * lax.rsqrt(lax.optimization_barrier(jnp.mean(as_float * as_float, axis=-1, keepdims=True)) + 1e-06) * gain

def mixer(layer_input, mixer_norm_gain, convolution_weight, convolution_bias, input_projection, step_size_projection, step_size_bias, log_decay_rates, mixer_skip_weight):
    length = layer_input.shape[0]
    normed = rms_scale(layer_input, mixer_norm_gain).astype(jnp.bfloat16)
    padded = jnp.concatenate([jnp.zeros((KCONV - 1, MODEL_DIM), jnp.bfloat16), normed], 0)
    convolved = convolution_bias
    for tap in range(KCONV):
        convolved = convolved + convolution_weight[tap] * padded[tap:tap + length].astype(jnp.float32)
    inner = jax.nn.silu(convolved)
    inner_b = inner.astype(jnp.bfloat16)
    projected = jnp.dot(inner_b, input_projection, preferred_element_type=jnp.float32)
    low_rank = projected[:, :RANK].astype(jnp.bfloat16)
    b_in = projected[:, RANK:RANK + NSTATE]
    c_out = projected[:, RANK + NSTATE:]
    step_size = jax.nn.softplus(jnp.dot(low_rank, step_size_projection, preferred_element_type=jnp.float32) + step_size_bias)
    decay_rates = -jnp.exp(log_decay_rates)

    def advance(state, row_items):
        dt_row, in_row, b_row, c_row = row_items
        state = jnp.exp(dt_row[:, None] * decay_rates) * state + (dt_row * in_row)[:, None] * b_row[None, :]
        return (state, lax.optimization_barrier(jnp.sum(state * c_row[None, :], axis=1)))
    _, scanned = lax.scan(advance, jnp.zeros((MODEL_DIM, NSTATE), jnp.float32), (step_size, inner, b_in, c_out))
    return (layer_input.astype(jnp.float32) + (scanned + mixer_skip_weight * inner)).astype(jnp.bfloat16)

def experts_ref(mixed_rows, expert_norm_gain, router, gate_weight, up_weight, down_weight, chosen_ids):
    length = mixed_rows.shape[0]
    moe_in = rms_scale(mixed_rows, expert_norm_gain).astype(jnp.bfloat16)
    logits = jnp.dot(moe_in, router, preferred_element_type=jnp.float32)
    first = jnp.take_along_axis(logits, chosen_ids[:, 0:1], 1)[:, 0]
    second = jnp.take_along_axis(logits, chosen_ids[:, 1:2], 1)[:, 0]
    weight_one = jax.nn.sigmoid(first - second)
    weight_two = 1.0 - weight_one
    route_weight = jnp.where(chosen_ids[:, 0] == 0, weight_one, jnp.where(chosen_ids[:, 1] == 0, weight_two, jnp.zeros_like(weight_one)))
    routed = ((chosen_ids[:, 0] == 0) | (chosen_ids[:, 1] == 0)).astype(jnp.int32)
    blocked = routed.reshape(N_SEQ, L_DEV)
    slot = (jnp.cumsum(blocked, 1) - blocked).reshape(-1).astype(jnp.int32)
    block_of = (jnp.arange(length, dtype=jnp.int32) // L_DEV).astype(jnp.int32)
    total_slots = N_SEQ * CAP
    target = jnp.where(routed == 1, block_of * CAP + slot, total_slots).astype(jnp.int32)
    table = jnp.full((total_slots + 1,), length, jnp.int32).at[target].set(jnp.arange(length, dtype=jnp.int32))[:total_slots]
    padded_in = jnp.concatenate([moe_in, jnp.zeros((1, MODEL_DIM), jnp.bfloat16)], 0)
    sectioned = jnp.take(padded_in, table, axis=0)
    width = FF // N_SEQ

    def slice_term(total, index):
        start = (index * width).astype(jnp.int32)
        gate_cols = lax.dynamic_slice_in_dim(gate_weight, start, width, 1)
        up_cols = lax.dynamic_slice_in_dim(up_weight, start, width, 1)
        down_rows = lax.dynamic_slice_in_dim(down_weight, start, width, 0)
        gate_part = jnp.dot(sectioned, gate_cols, preferred_element_type=jnp.float32)
        up_part = jnp.dot(sectioned, up_cols, preferred_element_type=jnp.float32)
        hidden = (jax.nn.silu(gate_part) * up_part).astype(jnp.bfloat16)
        partial_value = jnp.dot(hidden, down_rows, preferred_element_type=jnp.float32).astype(jnp.bfloat16)
        partial_value = lax.optimization_barrier(partial_value)
        return (total + partial_value.astype(jnp.float32), None)
    summed, _ = lax.scan(slice_term, jnp.zeros((total_slots, MODEL_DIM), jnp.float32), jnp.arange(N_SEQ, dtype=jnp.int32))
    expert_out = summed.astype(jnp.bfloat16)
    padded_out = jnp.concatenate([expert_out, jnp.zeros((1, MODEL_DIM), jnp.bfloat16)], 0)
    picked = jnp.take(padded_out, target, axis=0).astype(jnp.float32)
    combined = route_weight[:, None] * picked
    return (mixed_rows.astype(jnp.float32) + combined).astype(jnp.bfloat16)

def reference(input_in_transit, mixer_norm_gain, convolution_weight, convolution_bias, input_projection, step_size_projection, step_size_bias, log_decay_rates, mixer_skip_weight, expert_norm_gain, router, gate_weight, up_weight, down_weight, expert_index_table):
    present_value = [input_in_transit[section_index] for section_index in range(N_SECTION)]
    produced = present_value
    for step in range(STEPS):
        produced = []
        for section_index in range(N_SECTION):
            mixed_rows = mixer(present_value[section_index], mixer_norm_gain[section_index], convolution_weight[section_index], convolution_bias[section_index], input_projection[section_index], step_size_projection[section_index], step_size_bias[section_index], log_decay_rates[section_index], mixer_skip_weight[section_index])
            produced.append(experts_ref(mixed_rows, expert_norm_gain[section_index], router[section_index], gate_weight[section_index], up_weight[section_index], down_weight[section_index], expert_index_table[step, section_index]))
        present_value = [produced[(section_index - 1) % N_SECTION] for section_index in range(N_SECTION)]
    return jnp.stack(produced, 0)
```

```python
import functools

import jax
import jax.numpy as jnp
from jax import lax
from jax.experimental import pallas as pl
from jax.experimental.pallas import tpu as pltpu
from jax.sharding import PartitionSpec as P

STEPS = 2
ROWS = 128
WIDTH = 4096
NSTATE = 16
RANK = 256
SLOTS = 8
TILES = WIDTH // 128
GROUPS = 4
HALO = 8
NY, NX, NC = 4, 4, 2
NQ = NY * NX * NC
LOG2E = 1.4426950408889634
PAYLOAD = GROUPS * NSTATE * 8 + 2 * TILES
F32, BF16 = jnp.float32, jnp.bfloat16

VMEM = pl.BlockSpec(memory_space=pltpu.VMEM)
SMEM = pl.BlockSpec(memory_space=pltpu.SMEM)


def params():
    return pltpu.CompilerParams(vmem_limit_bytes=50 * 1024 * 1024)


def call(kernel, ins, outs, scratch=(), n_smem=0, flops=0, name=None):
    moved = sum(v.size * v.dtype.itemsize for v in ins) + sum(
        o.size * o.dtype.itemsize for o in outs
    )
    return pl.pallas_call(
        kernel,
        out_shape=outs,
        in_specs=[SMEM] * n_smem + [VMEM] * (len(ins) - n_smem),
        out_specs=[VMEM] * len(outs),
        scratch_shapes=list(scratch),
        compiler_params=params(),
        cost_estimate=pl.CostEstimate(flops=flops, bytes_accessed=moved, transcendentals=0),
        name=name,
    )(*ins)


def tile_of(j):
    return pl.ds(pl.multiple_of(j * 128, 128), 128)


def pre_kernel(fresh, *refs):
    if fresh:
        x_ref, halo_ref, gain_ref, taps_ref, bias_ref, inner_ref, rows = refs
    else:
        (x_ref, halo_ref, slot_ref, halo_slot_ref, out_ref, halo_out_ref,
         gain_ref, taps_ref, bias_ref, inner_ref, x_out_ref, rows) = refs
    chunk = 512
    total = jnp.zeros((HALO + ROWS, 128), F32)
    for j in range(WIDTH // chunk):
        cols = slice(j * chunk, (j + 1) * chunk)
        own = x_ref[:, cols].astype(F32)
        behind = halo_ref[:, cols].astype(F32)
        if not fresh:
            dims = (((0,), (0,)), ((), ()))
            own = own + lax.dot_general(
                slot_ref[...], out_ref[:, cols].astype(F32), dims,
                precision=lax.Precision.HIGHEST, preferred_element_type=F32)
            own = own.astype(BF16)
            x_out_ref[:, cols] = own
            own = own.astype(F32)
            add = lax.dot_general(
                halo_slot_ref[...], halo_out_ref[:, cols].astype(F32), dims,
                precision=lax.Precision.HIGHEST, preferred_element_type=F32)
            behind = (behind + add[ROWS - HALO :]).astype(BF16).astype(F32)
        both = jnp.concatenate([behind, own], 0)
        rows[:, cols] = both
        square = both * both
        for i in range(chunk // 128):
            total = total + square[:, i * 128 : (i + 1) * 128]
    scale = lax.rsqrt(jnp.sum(total, axis=1, keepdims=True) * (1.0 / WIDTH) + 1e-06)
    chunk = 256
    for j in range(WIDTH // chunk):
        cols = slice(j * chunk, (j + 1) * chunk)
        normed = (rows[:, cols] * scale * gain_ref[:, cols]).astype(BF16).astype(F32)
        rows[:, cols] = normed
        acc = bias_ref[:, cols]
        for k in range(4):
            first = HALO - 3 + k
            acc = acc + taps_ref[k : k + 1, cols] * rows[first : first + ROWS, cols]
        inner_ref[:, cols] = acc * jax.nn.sigmoid(acc)


def main_kernel(order_ref, inner_ref, w_ref, wdt_ref, bias_ref, a_ref,
                dt_ref, dtx_ref, b_ref, c_ref, payload_ref, state, steps):
    def project(r, acc):
        lhs = inner_ref[:, tile_of(order_ref[r])].astype(BF16)
        return acc + jnp.dot(lhs, w_ref[r], preferred_element_type=F32)

    projected = lax.fori_loop(
        0, NQ, project, jnp.zeros((ROWS, RANK + 2 * NSTATE), F32), unroll=4
    )
    low = projected[:, :RANK].astype(BF16)
    for n in range(NSTATE):
        for ref, at in ((b_ref, RANK), (c_ref, RANK + NSTATE)):
            column = projected[:, at + n : at + n + 1]
            ref[pl.ds(n, ROWS, stride=NSTATE), :] = jnp.broadcast_to(column, (ROWS, 128))

    def step_size(r, carry):
        q = order_ref[r]
        z = jnp.dot(low, wdt_ref[r], preferred_element_type=F32) + bias_ref[:, tile_of(q)]
        dt = jnp.maximum(z, 0.0) + jnp.log1p(jnp.exp(-jnp.abs(z)))
        g, s = q // 8, q % 8
        dt_ref[g, pl.ds(s, ROWS, stride=8), :] = dt
        dtx_ref[g, pl.ds(s, ROWS, stride=8), :] = dt * inner_ref[:, tile_of(q)]
        return carry

    lax.fori_loop(0, NQ, step_size, 0, unroll=2)

    def group(g, carry):
        a = [a_ref[pl.ds(pl.multiple_of(g * 128 + n * 8, 8), 8), :] for n in range(NSTATE)]

        def advance(t, hs):
            at = pl.ds(pl.multiple_of(t * 8, 8), 8)
            dt, dtx = dt_ref[g, at, :], dtx_ref[g, at, :]
            new = [
                jnp.exp2(dt * a[n]) * hs[n] + dtx * b_ref[pl.ds(t * NSTATE + n, 1), :]
                for n in range(NSTATE)
            ]
            return (*new, hs[NSTATE] + dt)

        hs = lax.fori_loop(
            0, ROWS, advance, tuple(jnp.zeros((8, 128), F32) for _ in range(NSTATE + 1)), unroll=4
        )
        for n in range(NSTATE):
            state[pl.ds(pl.multiple_of(g * 128 + n * 8, 8), 8), :] = hs[n]
        steps[pl.ds(pl.multiple_of(g * 8, 8), 8), :] = hs[NSTATE]
        return carry

    lax.fori_loop(0, GROUPS, group, 0)
    pack(payload_ref, state[...], steps[...])


def pack(ref, state, steps):
    n = GROUPS * NSTATE * 8
    ref[:n, :] = state.astype(BF16)
    high = steps.astype(BF16)
    ref[n : n + TILES, :] = high
    ref[n + TILES :, :] = (steps - high.astype(F32)).astype(BF16)


def unpack(ref):
    n = GROUPS * NSTATE * 8
    value = ref[...].astype(F32)
    return value[:n], value[n : n + TILES] + value[n + TILES :]


def decayed(a_ref, steps, state):
    s = steps.reshape(GROUPS, 1, 8, 128)
    a = a_ref[...].reshape(GROUPS, NSTATE, 8, 128)
    return jnp.exp2(a * s).reshape(GROUPS * NSTATE * 8, 128) * state


def chain(a_ref, earlier, later):
    return decayed(a_ref, later[1], earlier[0]) + later[0], earlier[1] + later[1]


def chip_kernel(place_ref, a_ref, pair_ref, payload_ref):
    core = place_ref[2]
    first = unpack(pair_ref.at[core])
    second = unpack(pair_ref.at[1 - core])
    pack(payload_ref, *chain(a_ref, first, second))


def prefix(a_ref, stack_ref, place, count, total):
    def hop(i, carry):
        mine, run = carry
        block = unpack(stack_ref.at[lax.rem(place - i + count, count)])
        new = chain(a_ref, run, block)
        before = i < place
        mine = tuple(jnp.where(before, u, v) for u, v in zip(new, mine))
        return mine, new

    zero = (jnp.zeros((GROUPS * NSTATE * 8, 128), F32), jnp.zeros((TILES, 128), F32))
    return lax.fori_loop(0, count if total else place, hop, (zero, zero))


def row_kernel(place_ref, a_ref, stack_ref, payload_ref, state_ref, steps_ref):
    mine, run = prefix(a_ref, stack_ref, place_ref[1], NX, True)
    pack(payload_ref, *run)
    state_ref[...], steps_ref[...] = mine


def scan_kernel(place_ref, a_ref, columns_ref, row_state_ref, row_steps_ref, pair_ref,
                dt_ref, dtx_ref, b_ref, c_ref, inner_ref, x_ref, skip_ref, gain_ref, router_ref, ids_ref,
                mixed_ref, slot_ref, sectioned_ref, state, out, moe):
    _, ahead = prefix(a_ref, columns_ref, place_ref[0], NY, False)
    ahead = chain(a_ref, ahead, (row_state_ref[...], row_steps_ref[...]))
    other = chain(a_ref, ahead, unpack(pair_ref.at[1]))
    state[...] = jnp.where(place_ref[2] == 1, other[0], ahead[0])

    def group(g, carry):
        a = [a_ref[pl.ds(pl.multiple_of(g * 128 + n * 8, 8), 8), :] for n in range(NSTATE)]

        def advance(t, hs):
            at = pl.ds(pl.multiple_of(t * 8, 8), 8)
            dt, dtx = dt_ref[g, at, :], dtx_ref[g, at, :]
            new, parts = [], []
            for n in range(NSTATE):
                row = pl.ds(t * NSTATE + n, 1)
                h = jnp.exp2(dt * a[n]) * hs[n] + dtx * b_ref[row, :]
                new.append(h)
                part = h * c_ref[row, :]
                if n < 4:
                    parts.append(part)
                else:
                    parts[n % 4] = parts[n % 4] + part
            out[g, at, :] = (parts[0] + parts[1]) + (parts[2] + parts[3])
            return tuple(new)

        start = tuple(
            state[pl.ds(pl.multiple_of(g * 128 + n * 8, 8), 8), :] for n in range(NSTATE)
        )
        lax.fori_loop(0, ROWS, advance, start, unroll=4)
        return carry

    lax.fori_loop(0, GROUPS, group, 0)

    total = jnp.zeros((ROWS, 128), F32)
    for j in range(TILES):
        cols = slice(j * 128, (j + 1) * 128)
        scanned = out[j // 8, pl.ds(j % 8, ROWS, stride=8), :]
        mixed = (
            x_ref[:, cols].astype(F32) + (scanned + skip_ref[:, cols] * inner_ref[:, cols])
        ).astype(BF16)
        mixed_ref[:, cols] = mixed
        mixed = mixed.astype(F32)
        total = total + mixed * mixed
    scale = lax.rsqrt(jnp.sum(total, axis=1, keepdims=True) * (1.0 / WIDTH) + 1e-06)
    for j in range(TILES // 2):
        cols = slice(j * 256, (j + 1) * 256)
        moe[:, cols] = (mixed_ref[:, cols].astype(F32) * scale * gain_ref[:, cols]).astype(BF16)
    logits = lax.dot_general(
        router_ref[...], moe[...], (((1,), (1,)), ((), ())), preferred_element_type=F32
    )
    one, two = ids_ref[0:1, :], ids_ref[1:2, :]
    expert = lax.broadcasted_iota(jnp.int32, (16, ROWS), 0)
    first = jnp.sum(jnp.where(expert == one, logits, 0.0), axis=0, keepdims=True)
    second = jnp.sum(jnp.where(expert == two, logits, 0.0), axis=0, keepdims=True)
    weight_one = jax.nn.sigmoid(first - second)
    weight = jnp.where(one == 0, weight_one, jnp.where(two == 0, 1.0 - weight_one, 0.0))
    routed = jnp.where((one == 0) | (two == 0), 1.0, 0.0)
    earlier = lax.broadcasted_iota(jnp.int32, (ROWS, ROWS), 0) < lax.broadcasted_iota(
        jnp.int32, (ROWS, ROWS), 1
    )
    ahead_of = jnp.dot(
        jnp.broadcast_to(routed, (8, ROWS)), jnp.where(earlier, 1.0, 0.0), preferred_element_type=F32
    )
    slot = lax.broadcasted_iota(jnp.int32, (SLOTS, ROWS), 0).astype(F32)
    chosen = jnp.where((ahead_of == slot) & (routed > 0.0), 1.0, 0.0)
    slot_ref[...] = chosen * weight
    sectioned_ref[...] = jnp.dot(
        chosen.astype(BF16), moe[...], preferred_element_type=F32
    ).astype(BF16)


def final_kernel(x_ref, slot_ref, out_ref, y_ref):
    dims = (((0,), (0,)), ((), ()))
    for j in range(WIDTH // 512):
        cols = slice(j * 512, (j + 1) * 512)
        add = lax.dot_general(
            slot_ref[...], out_ref[:, cols].astype(F32), dims,
            precision=lax.Precision.HIGHEST, preferred_element_type=F32)
        y_ref[:, cols] = (x_ref[:, cols].astype(F32) + add).astype(BF16)


def index(y, x, c):
    return (y % NY) * NX * NC + (x % NX) * NC + c % NC


def shifted(block, dy, dx, dc):
    route = [
        (index(y, x, c), index(y + dy, x + dx, c + dc))
        for y in range(NY)
        for x in range(NX)
        for c in range(NC)
    ]
    return lax.ppermute(block, "seq", route)


def onward(block, sections, distance):
    route = [
        (s * NQ + q, (s + 1) % sections * NQ + q + distance)
        for s in range(sections)
        for q in range(NQ)
        if q + distance < NQ
    ]
    return lax.ppermute(block, ("section", "seq"), route)


def along_x(block):
    return jnp.stack([block] + [shifted(block, 0, k, 0) for k in range(1, NX)])


def along_y(block):
    return jnp.stack([block] + [shifted(block, k, 0, 0) for k in range(1, NY)])


def along_core(block):
    return jnp.stack([block, shifted(block, 0, 0, 1)])


def body(
    input_in_transit,
    mixer_norm_gain,
    convolution_weight,
    convolution_bias,
    input_projection,
    step_size_projection,
    step_size_bias,
    log_decay_rates,
    mixer_skip_weight,
    expert_norm_gain,
    router,
    gate_weight,
    up_weight,
    down_weight,
    expert_index_table,
):
    sections = lax.axis_size("section")
    q = lax.axis_index("seq")
    y, x, c = q // (NX * NC), q // NC % NX, q % NC
    place = jnp.stack([y, x, c]).astype(jnp.int32)
    sds = jax.ShapeDtypeStruct

    rates = (-LOG2E) * jnp.exp(log_decay_rates[0])
    rates = rates.reshape(GROUPS, 8, 128, NSTATE).transpose(0, 3, 1, 2)
    rates = rates.reshape(GROUPS * NSTATE * 8, 128)
    router_t = router[0].T
    ids = expert_index_table[:, 0].transpose(0, 2, 1)

    w = along_core(along_y(along_x(input_projection[0])))
    w = w.reshape(NQ, ROWS, RANK + 2 * NSTATE)
    wdt = along_core(along_x(along_y(step_size_projection[0])))
    wdt = wdt.reshape(NC, NX, NY, RANK, 128).transpose(0, 2, 1, 3, 4).reshape(NQ, RANK, 128)
    kc, ky, kx = jnp.meshgrid(jnp.arange(NC), jnp.arange(NY), jnp.arange(NX), indexing="ij")
    order = (y - ky) % NY * (NX * NC) + (x - kx) % NX * NC + (c + kc) % NC
    order = order.reshape(NQ).astype(jnp.int32)

    present = input_in_transit[0]
    behind = lax.ppermute(present[ROWS - HALO :], "seq", [(i, i + 1) for i in range(NQ - 1)])
    extra = None
    for step in range(STEPS):
        gains = [mixer_norm_gain, convolution_weight[0], convolution_bias]
        inner_shape = sds((ROWS, WIDTH), F32)
        rows = pltpu.VMEM((HALO + ROWS, WIDTH), F32)
        if step == 0:
            (inner,) = call(
                functools.partial(pre_kernel, True), [present, behind, *gains], [inner_shape], [rows],
                name="pre")
        else:
            inner, present = call(
                functools.partial(pre_kernel, False), [present, behind, *extra, *gains],
                [inner_shape, sds((ROWS, WIDTH), BF16)], [rows], name="pre_next")
        wide = sds((GROUPS, ROWS * 8, 128), F32)
        tall = sds((ROWS * NSTATE, 128), F32)
        packed = sds((PAYLOAD, 128), BF16)
        states = pltpu.VMEM((GROUPS * NSTATE * 8, 128), F32)
        dt, dtx, b, c_out, payload = call(
            main_kernel, [order, inner, w, wdt, step_size_bias, rates],
            [wide, wide, tall, tall, packed], [states, pltpu.VMEM((TILES, 128), F32)], n_smem=1,
            name="project_and_end")
        pair = along_core(payload)
        (chip,) = call(chip_kernel, [place, rates, pair], [packed], n_smem=1, name="chip")
        row, row_state, row_steps = call(
            row_kernel, [place, rates, along_x(chip)],
            [packed, sds((GROUPS * NSTATE * 8, 128), F32), sds((TILES, 128), F32)], n_smem=1,
            name="row")
        mixed, slots, sectioned = call(
            scan_kernel,
            [place, rates, along_y(row), row_state, row_steps, pair, dt, dtx, b, c_out, inner, present,
             mixer_skip_weight, expert_norm_gain, router_t, ids[step]],
            [sds((ROWS, WIDTH), BF16), sds((SLOTS, ROWS), F32), sds((SLOTS, WIDTH), BF16)],
            [states, pltpu.VMEM((GROUPS, ROWS * 8, 128), F32), pltpu.VMEM((ROWS, WIDTH), BF16)],
            n_smem=1, name="scan")
        last = step + 1 == STEPS
        if not last:
            next_mixed = onward(mixed, sections, 0)
            next_behind = onward(mixed[ROWS - HALO :], sections, 1)
            next_slots = onward(slots, sections, 0)
            next_slots_behind = onward(slots, sections, 1)
        gathered = along_core(along_y(along_x(sectioned))).reshape(NQ * SLOTS, WIDTH)
        gate = jnp.dot(gathered, gate_weight[0], preferred_element_type=F32)
        up = jnp.dot(gathered, up_weight[0], preferred_element_type=F32)
        hidden = (jax.nn.silu(gate) * up).astype(BF16)
        terms = jnp.dot(hidden, down_weight[0], preferred_element_type=F32).astype(BF16)
        terms = terms.reshape(NC, NY, NX, SLOTS, WIDTH)
        own = terms[0].astype(F32) + shifted(terms[1], 0, 0, 1).astype(F32)
        own = own.astype(BF16)
        total = own[0].astype(F32)
        for k in range(1, NY):
            total = total + shifted(own[k], -k, 0, 0).astype(F32)
        own = total.astype(BF16)
        total = own[0].astype(F32)
        for k in range(1, NX):
            total = total + shifted(own[k], 0, -k, 0).astype(F32)
        expert_out = total.astype(BF16)
        if last:
            (produced,) = call(
                final_kernel, [mixed, slots, expert_out], [sds((ROWS, WIDTH), BF16)], name="final"
            )
        else:
            extra = [
                next_slots, next_slots_behind, onward(expert_out, sections, 0),
                onward(expert_out, sections, 1),
            ]
            present, behind = next_mixed, next_behind
    return produced[None]


def solution(mesh):
    return jax.shard_map(
        body,
        mesh=mesh,
        in_specs=(
            P("section", "seq", None),
            P("section", None),
            P("section", None, None),
            P("section", None),
            P("section", "seq", None),
            P("section", None, "seq"),
            P("section", None),
            P("section", None, None),
            P("section", None),
            P("section", None),
            P("section", None, None),
            P("section", None, "seq"),
            P("section", None, "seq"),
            P("section", "seq", None),
            P(None, "section", "seq", None),
        ),
        out_specs=P("section", "seq", None),
        check_vma=False,
    )
```

```python
import functools

import jax
import jax.numpy as jnp
from jax import lax
from jax.experimental import pallas as pl
from jax.experimental.pallas import tpu as pltpu
from jax.sharding import PartitionSpec as P

STEPS = 2
ROWS = 128
WIDTH = 4096
NSTATE = 16
RANK = 256
SLOTS = 8
TILES = WIDTH // 128
GROUPS = 4
HALO = 16
EXTRA = 128
NY, NX, NC = 4, 4, 2
NQ = NY * NX * NC
LOG2E = 1.4426950408889634
PAYLOAD = GROUPS * NSTATE * 8 + 2 * TILES
F32, BF16 = jnp.float32, jnp.bfloat16

VMEM = pl.BlockSpec(memory_space=pltpu.VMEM)
SMEM = pl.BlockSpec(memory_space=pltpu.SMEM)


def call(kernel, ins, outs, scratch=(), n_smem=0, flops=0, name=None, mib=16):
    moved = sum(v.size * v.dtype.itemsize for v in ins) + sum(
        o.size * o.dtype.itemsize for o in outs
    )
    return pl.pallas_call(
        kernel,
        out_shape=outs,
        in_specs=[SMEM] * n_smem + [VMEM] * (len(ins) - n_smem),
        out_specs=[VMEM] * len(outs),
        scratch_shapes=list(scratch),
        compiler_params=pltpu.CompilerParams(vmem_limit_bytes=mib * 1024 * 1024),
        cost_estimate=pl.CostEstimate(flops=flops, bytes_accessed=moved, transcendentals=0),
        name=name,
    )(*ins)


def tile_of(j):
    return pl.ds(pl.multiple_of(j * 128, 128), 128)


def slot_rows(slots, out_ref, cols):
    out = out_ref[:, cols].astype(F32)
    out = jnp.concatenate([out, out], 0).astype(BF16)
    return lax.dot_general(slots, out, (((0,), (0,)), ((), ())), preferred_element_type=F32)


def pre_kernel(fresh, *refs):
    if fresh:
        x_ref, halo_ref, gain_ref, taps_ref, bias_ref, inner_ref, rows = refs
    else:
        (x_ref, halo_ref, out_ref, halo_out_ref,
         gain_ref, taps_ref, bias_ref, inner_ref, x_out_ref, rows) = refs
        slots, halo_slots = x_ref[:16, WIDTH:], halo_ref[:, WIDTH:]
    chunk = 512
    total = jnp.zeros((HALO + ROWS, 128), F32)
    for j in range(WIDTH // chunk):
        cols = slice(j * chunk, (j + 1) * chunk)
        own = x_ref[:, cols].astype(F32)
        behind = halo_ref[:, cols].astype(F32)
        if not fresh:
            own = (own + slot_rows(slots, out_ref, cols)).astype(BF16)
            x_out_ref[:, cols] = own
            own = own.astype(F32)
            add = slot_rows(halo_slots, halo_out_ref, cols)
            behind = (behind + add[ROWS - HALO :]).astype(BF16).astype(F32)
        both = jnp.concatenate([behind, own], 0)
        rows[:, cols] = both
        square = both * both
        for i in range(chunk // 128):
            total = total + square[:, i * 128 : (i + 1) * 128]
    scale = lax.rsqrt(jnp.sum(total, axis=1, keepdims=True) * (1.0 / WIDTH) + 1e-06)
    chunk = 256
    for j in range(WIDTH // chunk):
        cols = slice(j * chunk, (j + 1) * chunk)
        normed = (rows[:, cols] * scale * gain_ref[:, cols]).astype(BF16).astype(F32)
        rows[:, cols] = normed
        acc = bias_ref[:, cols]
        for k in range(4):
            first = HALO - 3 + k
            acc = acc + taps_ref[k : k + 1, cols] * rows[first : first + ROWS, cols]
        inner_ref[:, cols] = acc * jax.nn.sigmoid(acc)


def softplus(z):
    e = jnp.exp(-jnp.abs(z))
    small = e * (1.0 - e * (0.5 - e * (1.0 / 3.0)))
    return jnp.maximum(z, 0.0) + jnp.where(e < 0.005, small, jnp.log(1.0 + e))


def main_kernel(order_ref, inner_ref, bias_ref, a_ref, *refs):
    w, wdt = refs[: NC * NY], refs[NC * NY : NC * (NY + NX)]
    dt_ref, dtx_ref, b_ref, c_ref, payload_ref, state, steps = refs[NC * (NY + NX) :]

    def place(ky, kx):
        return [order_ref[(kc * NY + ky) * NX + kx] for kc in range(NC)]

    projected = jnp.zeros((ROWS, RANK + 2 * NSTATE), F32)
    for ky in range(NY):
        for kx in range(NX):
            lhs = [inner_ref[:, tile_of(q)].astype(BF16) for q in place(ky, kx)]
            rhs = [w[kc * NY + ky][kx] for kc in range(NC)]
            projected = projected + lax.dot_general(
                jnp.concatenate(lhs, 1), jnp.concatenate(rhs, 1), (((1,), (1,)), ((), ())),
                preferred_element_type=F32)
    low = projected[:, :RANK].astype(BF16)
    for n in range(NSTATE):
        for ref, at in ((b_ref, RANK), (c_ref, RANK + NSTATE)):
            column = projected[:, at + n : at + n + 1]
            ref[pl.ds(n, ROWS, stride=NSTATE), :] = jnp.broadcast_to(column, (ROWS, 128))

    for kx in range(NX):
        for ky in range(NY):
            rhs = jnp.concatenate([wdt[kc * NX + kx][ky] for kc in range(NC)], 1)
            both = jnp.dot(low, rhs, preferred_element_type=F32)
            for kc, q in enumerate(place(ky, kx)):
                dt = softplus(both[:, kc * 128 : (kc + 1) * 128] + bias_ref[:, tile_of(q)])
                g, s = q // 8, q % 8
                dt_ref[g, pl.ds(s, ROWS, stride=8), :] = dt
                dtx_ref[g, pl.ds(s, ROWS, stride=8), :] = dt * inner_ref[:, tile_of(q)]

    def group(g, carry):
        a = [a_ref[pl.ds(pl.multiple_of(g * 128 + n * 8, 8), 8), :] for n in range(NSTATE)]

        def advance(t, hs):
            at = pl.ds(pl.multiple_of(t * 8, 8), 8)
            dt, dtx = dt_ref[g, at, :], dtx_ref[g, at, :]
            new = [
                jnp.exp2(dt * a[n]) * hs[n] + dtx * b_ref[pl.ds(t * NSTATE + n, 1), :]
                for n in range(NSTATE)
            ]
            return (*new, hs[NSTATE] + dt)

        hs = lax.fori_loop(
            0, ROWS, advance, tuple(jnp.zeros((8, 128), F32) for _ in range(NSTATE + 1)), unroll=8
        )
        for n in range(NSTATE):
            state[pl.ds(pl.multiple_of(g * 128 + n * 8, 8), 8), :] = hs[n]
        steps[pl.ds(pl.multiple_of(g * 8, 8), 8), :] = hs[NSTATE]
        return carry

    lax.fori_loop(0, GROUPS, group, 0)
    pack(payload_ref, state[...], steps[...])


def pack(ref, state, steps):
    n = GROUPS * NSTATE * 8
    ref[:n, :] = state.astype(BF16)
    high = steps.astype(BF16)
    ref[n : n + TILES, :] = high
    ref[n + TILES :, :] = (steps - high.astype(F32)).astype(BF16)


def unpack(ref):
    n = GROUPS * NSTATE * 8
    value = ref[...].astype(F32)
    return value[:n], value[n : n + TILES] + value[n + TILES :]


def decayed(a_ref, steps, state):
    s = steps.reshape(GROUPS, 1, 8, 128)
    a = a_ref[...].reshape(GROUPS, NSTATE, 8, 128)
    return jnp.exp2(a * s).reshape(GROUPS * NSTATE * 8, 128) * state


def chain(a_ref, earlier, later):
    return decayed(a_ref, later[1], earlier[0]) + later[0], earlier[1] + later[1]


def chip_kernel(place_ref, a_ref, own_ref, other_ref, payload_ref):
    own, other = unpack(own_ref), unpack(other_ref)
    swap = place_ref[2] == 1
    first = tuple(jnp.where(swap, b, a) for a, b in zip(own, other))
    second = tuple(jnp.where(swap, a, b) for a, b in zip(own, other))
    pack(payload_ref, *chain(a_ref, first, second))


def prefix(a_ref, stack, refs, place, total):
    count = len(refs)
    for k, ref in enumerate(refs):
        stack[k] = ref[...]

    def hop(i, carry):
        mine, run = carry
        block = unpack(stack.at[lax.rem(place - i + count, count)])
        new = chain(a_ref, run, block)
        before = i < place
        mine = tuple(jnp.where(before, u, v) for u, v in zip(new, mine))
        return mine, new

    zero = (jnp.zeros((GROUPS * NSTATE * 8, 128), F32), jnp.zeros((TILES, 128), F32))
    return lax.fori_loop(0, count if total else place, hop, (zero, zero))


def row_kernel(place_ref, a_ref, *refs):
    blocks, (payload_ref, state_ref, steps_ref, stack) = refs[:NX], refs[NX:]
    mine, run = prefix(a_ref, stack, blocks, place_ref[1], True)
    pack(payload_ref, *run)
    state_ref[...], steps_ref[...] = mine


def scan_kernel(place_ref, a_ref, *refs):
    columns, refs = refs[:NY], refs[NY:]
    (row_state_ref, row_steps_ref, other_ref,
     dt_ref, dtx_ref, b_ref, c_ref, inner_ref, x_ref, skip_ref, gain_ref, router_ref, ids_ref,
     mixed_ref, halo_ref, sectioned_ref, state, out, moe, stack) = refs
    _, ahead = prefix(a_ref, stack, columns, place_ref[0], False)
    ahead = chain(a_ref, ahead, (row_state_ref[...], row_steps_ref[...]))
    other = chain(a_ref, ahead, unpack(other_ref))
    state[...] = jnp.where(place_ref[2] == 1, other[0], ahead[0])

    def group(g, carry):
        a = [a_ref[pl.ds(pl.multiple_of(g * 128 + n * 8, 8), 8), :] for n in range(NSTATE)]

        def advance(t, hs):
            at = pl.ds(pl.multiple_of(t * 8, 8), 8)
            dt, dtx = dt_ref[g, at, :], dtx_ref[g, at, :]
            new, parts = [], []
            for n in range(NSTATE):
                row = pl.ds(t * NSTATE + n, 1)
                h = jnp.exp2(dt * a[n]) * hs[n] + dtx * b_ref[row, :]
                new.append(h)
                part = h * c_ref[row, :]
                if n < 4:
                    parts.append(part)
                else:
                    parts[n % 4] = parts[n % 4] + part
            out[g, at, :] = (parts[0] + parts[1]) + (parts[2] + parts[3])
            return tuple(new)

        start = tuple(
            state[pl.ds(pl.multiple_of(g * 128 + n * 8, 8), 8), :] for n in range(NSTATE)
        )
        lax.fori_loop(0, ROWS, advance, start, unroll=8)
        return carry

    lax.fori_loop(0, GROUPS, group, 0)

    total = jnp.zeros((ROWS, 128), F32)
    for j in range(TILES):
        cols = slice(j * 128, (j + 1) * 128)
        scanned = out[j // 8, pl.ds(j % 8, ROWS, stride=8), :]
        mixed = (
            x_ref[:, cols].astype(F32) + (scanned + skip_ref[:, cols] * inner_ref[:, cols])
        ).astype(BF16)
        mixed_ref[:, cols] = mixed
        halo_ref[:, cols] = mixed[ROWS - HALO :]
        mixed = mixed.astype(F32)
        total = total + mixed * mixed
    scale = lax.rsqrt(jnp.sum(total, axis=1, keepdims=True) * (1.0 / WIDTH) + 1e-06)
    for j in range(TILES // 2):
        cols = slice(j * 256, (j + 1) * 256)
        moe[:, cols] = (mixed_ref[:, cols].astype(F32) * scale * gain_ref[:, cols]).astype(BF16)
    logits = lax.dot_general(
        router_ref[...], moe[...], (((1,), (1,)), ((), ())), preferred_element_type=F32
    )
    one, two = ids_ref[0:1, :], ids_ref[1:2, :]
    expert = lax.broadcasted_iota(jnp.int32, (16, ROWS), 0)
    first = jnp.sum(jnp.where(expert == one, logits, 0.0), axis=0, keepdims=True)
    second = jnp.sum(jnp.where(expert == two, logits, 0.0), axis=0, keepdims=True)
    weight_one = jax.nn.sigmoid(first - second)
    weight = jnp.where(one == 0, weight_one, jnp.where(two == 0, 1.0 - weight_one, 0.0))
    routed = jnp.where((one == 0) | (two == 0), 1.0, 0.0)
    earlier = lax.broadcasted_iota(jnp.int32, (ROWS, ROWS), 0) < lax.broadcasted_iota(
        jnp.int32, (ROWS, ROWS), 1
    )
    ahead_of = jnp.dot(
        jnp.broadcast_to(routed, (8, ROWS)), jnp.where(earlier, 1.0, 0.0), preferred_element_type=F32
    )
    slot = lax.broadcasted_iota(jnp.int32, (SLOTS, ROWS), 0).astype(F32)
    chosen = jnp.where((ahead_of == slot) & (routed > 0.0), 1.0, 0.0)
    weights = chosen * weight
    high = weights.astype(BF16).astype(F32)
    slots = jnp.concatenate([high, weights - high], 0).astype(BF16)
    mixed_ref[:16, WIDTH:] = slots
    mixed_ref[16:, WIDTH:] = jnp.zeros((ROWS - 16, EXTRA), BF16)
    halo_ref[:, WIDTH:] = slots
    sectioned_ref[...] = jnp.dot(
        chosen.astype(BF16), moe[...], preferred_element_type=F32
    ).astype(BF16)


def final_kernel(x_ref, out_ref, y_ref):
    slots = x_ref[:16, WIDTH:]
    for j in range(WIDTH // 512):
        cols = slice(j * 512, (j + 1) * 512)
        y_ref[:, cols] = (x_ref[:, cols].astype(F32) + slot_rows(slots, out_ref, cols)).astype(BF16)


def expert_kernel(*refs):
    pieces, refs = refs[: NC * NY], refs[NC * NY :]
    gate_ref, up_ref, down_ref, own_ref, other_ref, xs = refs
    rows = NX * SLOTS
    for k, piece in enumerate(pieces):
        xs[k * rows : (k + 1) * rows, :] = piece[...]
    gate = jnp.dot(xs[...], gate_ref[...], preferred_element_type=F32)
    up = jnp.dot(xs[...], up_ref[...], preferred_element_type=F32)
    hidden = (gate * jax.nn.sigmoid(gate) * up).astype(BF16)
    half = NY * rows
    for j in range(WIDTH // 512):
        cols = slice(j * 512, (j + 1) * 512)
        terms = jnp.dot(hidden, down_ref[:, cols], preferred_element_type=F32).astype(BF16)
        own_ref[:, cols] = terms[:half]
        other_ref[:, cols] = terms[half:]


def sum_kernel(count, *refs):
    ins, outs = refs[:count], refs[count:]
    rows = outs[0].shape[0]
    for j in range(WIDTH // 512):
        cols = slice(j * 512, (j + 1) * 512)
        total = ins[0][:, cols].astype(F32)
        for ref in ins[1:]:
            total = total + ref[:, cols].astype(F32)
        for k, ref in enumerate(outs):
            ref[:, cols] = total[k * rows : (k + 1) * rows].astype(BF16)


def index(y, x, c):
    return (y % NY) * NX * NC + (x % NX) * NC + c % NC


def shifted(block, dy, dx, dc):
    route = [
        (index(y, x, c), index(y + dy, x + dx, c + dc))
        for y in range(NY)
        for x in range(NX)
        for c in range(NC)
    ]
    return lax.ppermute(block, "seq", route)


def onward(block, sections, distance):
    route = [
        (s * NQ + q, (s + 1) % sections * NQ + q + distance)
        for s in range(sections)
        for q in range(NQ)
        if q + distance < NQ
    ]
    return lax.ppermute(block, ("section", "seq"), route)


def along_x(block):
    return [block] + [shifted(block, 0, k, 0) for k in range(1, NX)]


def along_y(block):
    return [block] + [shifted(block, k, 0, 0) for k in range(1, NY)]


def along_core(blocks):
    return list(blocks) + [shifted(block, 0, 0, 1) for block in blocks]


def body(
    input_in_transit,
    mixer_norm_gain,
    convolution_weight,
    convolution_bias,
    input_projection,
    step_size_projection,
    step_size_bias,
    log_decay_rates,
    mixer_skip_weight,
    expert_norm_gain,
    router,
    gate_weight,
    up_weight,
    down_weight,
    expert_index_table,
):
    sections = lax.axis_size("section")
    q = lax.axis_index("seq")
    y, x, c = q // (NX * NC), q // NC % NX, q % NC
    place = jnp.stack([y, x, c]).astype(jnp.int32)
    sds = jax.ShapeDtypeStruct

    rates = (-LOG2E) * jnp.exp(log_decay_rates[0])
    rates = rates.reshape(GROUPS, 8, 128, NSTATE).transpose(0, 3, 1, 2)
    rates = rates.reshape(GROUPS * NSTATE * 8, 128)
    router_t = router[0].T
    ids = expert_index_table[:, 0].transpose(0, 2, 1)

    kc, ky, kx = jnp.meshgrid(jnp.arange(NC), jnp.arange(NY), jnp.arange(NX), indexing="ij")
    order = (y - ky) % NY * (NX * NC) + (x - kx) % NX * NC + (c + kc) % NC
    order = order.reshape(NQ).astype(jnp.int32)

    present = input_in_transit[0]
    behind = lax.ppermute(present[ROWS - HALO :], "seq", [(i, i + 1) for i in range(NQ - 1)])
    gains = [mixer_norm_gain, convolution_weight[0], convolution_bias]
    inner_shape = sds((ROWS, WIDTH), F32)
    rows = pltpu.VMEM((HALO + ROWS, WIDTH), F32)

    w = jnp.stack(along_x(input_projection[0].T))
    wdt = jnp.stack(along_y(step_size_projection[0]))
    (inner,) = call(
        functools.partial(pre_kernel, True), [present, behind, *gains], [inner_shape], [rows], name="pre"
    )
    w, wdt, inner, rates, order, place, router_t, ids = lax.optimization_barrier(
        (w, wdt, inner, rates, order, place, router_t, ids)
    )
    w = along_core(along_y(w))
    wdt = along_core(along_x(wdt))

    handed = None
    for step in range(STEPS):
        if step:
            inner, present = call(
                functools.partial(pre_kernel, False), [*handed, *gains],
                [inner_shape, sds((ROWS, WIDTH), BF16)], [rows], name="pre_next")
        wide = sds((GROUPS, ROWS * 8, 128), F32)
        tall = sds((ROWS * NSTATE, 128), F32)
        packed = sds((PAYLOAD, 128), BF16)
        states = pltpu.VMEM((GROUPS * NSTATE * 8, 128), F32)
        stack = pltpu.VMEM((NX, PAYLOAD, 128), BF16)
        dt, dtx, b, c_out, payload = call(
            main_kernel, [order, inner, step_size_bias, rates, *w, *wdt],
            [wide, wide, tall, tall, packed], [states, pltpu.VMEM((TILES, 128), F32)], n_smem=1,
            name="project_and_end", mib=24)
        other = shifted(payload, 0, 0, 1)
        (chip,) = call(chip_kernel, [place, rates, payload, other], [packed], n_smem=1, name="chip", mib=8)
        row, row_state, row_steps = call(
            row_kernel, [place, rates, *along_x(chip)],
            [packed, sds((GROUPS * NSTATE * 8, 128), F32), sds((TILES, 128), F32)], [stack], n_smem=1,
            name="row", mib=8)
        mixed, halo, sectioned = call(
            scan_kernel,
            [place, rates, *along_y(row), row_state, row_steps, other, dt, dtx, b, c_out, inner, present,
             mixer_skip_weight, expert_norm_gain, router_t, ids[step]],
            [sds((ROWS, WIDTH + EXTRA), BF16), sds((HALO, WIDTH + EXTRA), BF16), sds((SLOTS, WIDTH), BF16)],
            [states, pltpu.VMEM((GROUPS, ROWS * 8, 128), F32), pltpu.VMEM((ROWS, WIDTH), BF16), stack],
            n_smem=1, name="scan", mib=24)
        last = step + 1 == STEPS
        if not last:
            handed = [onward(mixed, sections, 0), onward(halo, sections, 1)]
        gathered = jnp.concatenate(along_x(sectioned), 0)
        gathered = along_core(along_y(gathered))
        half = sds((ROWS, WIDTH), BF16)
        own, others = call(
            expert_kernel, [*gathered, gate_weight[0], up_weight[0], down_weight[0]], [half, half],
            [pltpu.VMEM((NQ * SLOTS, WIDTH), BF16)], name="expert", mib=32)
        own = call(
            functools.partial(sum_kernel, NC), [own, shifted(others, 0, 0, 1)],
            [sds((NX * SLOTS, WIDTH), BF16)] * NY, name="sum_core", mib=8)
        own = call(
            functools.partial(sum_kernel, NY), [own[0]] + [shifted(own[k], -k, 0, 0) for k in range(1, NY)],
            [sds((SLOTS, WIDTH), BF16)] * NX, name="sum_y", mib=8)
        (expert_out,) = call(
            functools.partial(sum_kernel, NX), [own[0]] + [shifted(own[k], 0, -k, 0) for k in range(1, NX)],
            [sds((SLOTS, WIDTH), BF16)], name="sum_x", mib=8)
        if last:
            (produced,) = call(
                final_kernel, [mixed, expert_out], [sds((ROWS, WIDTH), BF16)], name="final", mib=8
            )
        else:
            handed += [onward(expert_out, sections, 0), onward(expert_out, sections, 1)]
    return produced[None]


def solution(mesh):
    return jax.shard_map(
        body,
        mesh=mesh,
        in_specs=(
            P("section", "seq", None),
            P("section", None),
            P("section", None, None),
            P("section", None),
            P("section", "seq", None),
            P("section", None, "seq"),
            P("section", None),
            P("section", None, None),
            P("section", None),
            P("section", None),
            P("section", None, None),
            P("section", None, "seq"),
            P("section", None, "seq"),
            P("section", "seq", None),
            P(None, "section", "seq", None),
        ),
        out_specs=P("section", "seq", None),
        check_vma=False,
    )
```

```python
import functools

import jax
import jax.numpy as jnp
from jax import lax
from jax.experimental import pallas as pl
from jax.experimental.pallas import tpu as pltpu
from jax.sharding import PartitionSpec as P

STEPS = 2
ROWS = 128
WIDTH = 4096
NSTATE = 16
RANK = 256
SLOTS = 8
TILES = WIDTH // 128
GROUPS = 4
HALO = 16
EXTRA = 128
NY, NX, NC = 4, 4, 2
NQ = NY * NX * NC
LOG2E = 1.4426950408889634
HALF = GROUPS // 2 * NSTATE * 8
STEPPED = TILES // 2
PAYLOAD = HALF + 2 * STEPPED
F32, BF16 = jnp.float32, jnp.bfloat16

VMEM = pl.BlockSpec(memory_space=pltpu.VMEM)
SMEM = pl.BlockSpec(memory_space=pltpu.SMEM)


def call(kernel, ins, outs, scratch=(), n_smem=0, flops=0, name=None, mib=16):
    moved = sum(v.size * v.dtype.itemsize for v in ins) + sum(
        o.size * o.dtype.itemsize for o in outs
    )
    return pl.pallas_call(
        kernel,
        out_shape=outs,
        in_specs=[SMEM] * n_smem + [VMEM] * (len(ins) - n_smem),
        out_specs=[VMEM] * len(outs),
        scratch_shapes=list(scratch),
        compiler_params=pltpu.CompilerParams(vmem_limit_bytes=mib * 1024 * 1024),
        cost_estimate=pl.CostEstimate(flops=flops, bytes_accessed=moved, transcendentals=0),
        name=name,
    )(*ins)


def tile_of(j):
    return pl.ds(pl.multiple_of(j * 128, 128), 128)


def slot_rows(slots, out_ref, cols):
    out = out_ref[:, cols].astype(F32)
    out = jnp.concatenate([out, out], 0).astype(BF16)
    return lax.dot_general(slots, out, (((0,), (0,)), ((), ())), preferred_element_type=F32)


def pre_kernel(fresh, *refs):
    if fresh:
        x_ref, halo_ref, gain_ref, taps_ref, bias_ref, inner_ref, rows = refs
    else:
        (x_ref, halo_ref, out_ref, halo_out_ref,
         gain_ref, taps_ref, bias_ref, inner_ref, x_out_ref, rows) = refs
        slots, halo_slots = x_ref[:16, WIDTH:], halo_ref[:, WIDTH:]
    chunk = 512
    total = jnp.zeros((HALO + ROWS, 128), F32)
    for j in range(WIDTH // chunk):
        cols = slice(j * chunk, (j + 1) * chunk)
        own = x_ref[:, cols].astype(F32)
        behind = halo_ref[:, cols].astype(F32)
        if not fresh:
            own = (own + slot_rows(slots, out_ref, cols)).astype(BF16)
            x_out_ref[:, cols] = own
            own = own.astype(F32)
            add = slot_rows(halo_slots, halo_out_ref, cols)
            behind = (behind + add[ROWS - HALO :]).astype(BF16).astype(F32)
        both = jnp.concatenate([behind, own], 0)
        rows[:, cols] = both
        square = both * both
        for i in range(chunk // 128):
            total = total + square[:, i * 128 : (i + 1) * 128]
    scale = lax.rsqrt(jnp.sum(total, axis=1, keepdims=True) * (1.0 / WIDTH) + 1e-06)
    chunk = 256
    for j in range(WIDTH // chunk):
        cols = slice(j * chunk, (j + 1) * chunk)
        normed = (rows[:, cols] * scale * gain_ref[:, cols]).astype(BF16).astype(F32)
        rows[:, cols] = normed
        acc = bias_ref[:, cols]
        for k in range(4):
            first = HALO - 3 + k
            acc = acc + taps_ref[k : k + 1, cols] * rows[first : first + ROWS, cols]
        inner_ref[:, cols] = acc * jax.nn.sigmoid(acc)


def softplus(z):
    e = jnp.exp(-jnp.abs(z))
    small = e * (1.0 - e * (0.5 - e * (1.0 / 3.0)))
    return jnp.maximum(z, 0.0) + jnp.where(e < 0.005, small, jnp.log(1.0 + e))


def main_kernel(order_ref, inner_ref, bias_ref, a_ref, *refs):
    w, wdt = refs[: NC * NY], refs[NC * NY : NC * (NY + NX)]
    dt_ref, dtx_ref, b_ref, c_ref, payload_ref, state, steps = refs[NC * (NY + NX) :]

    def place(ky, kx):
        return [order_ref[(kc * NY + ky) * NX + kx] for kc in range(NC)]

    projected = jnp.zeros((ROWS, RANK + 2 * NSTATE), F32)
    for ky in range(NY):
        for kx in range(NX):
            lhs = [inner_ref[:, tile_of(q)].astype(BF16) for q in place(ky, kx)]
            rhs = [w[kc * NY + ky][kx] for kc in range(NC)]
            projected = projected + lax.dot_general(
                jnp.concatenate(lhs, 1), jnp.concatenate(rhs, 1), (((1,), (1,)), ((), ())),
                preferred_element_type=F32)
    low = projected[:, :RANK].astype(BF16)
    for n in range(NSTATE):
        for ref, at in ((b_ref, RANK), (c_ref, RANK + NSTATE)):
            column = projected[:, at + n : at + n + 1]
            ref[pl.ds(n, ROWS, stride=NSTATE), :] = jnp.broadcast_to(column, (ROWS, 128))

    for kx in range(NX):
        for ky in range(NY):
            rhs = jnp.concatenate([wdt[kc * NX + kx][ky] for kc in range(NC)], 1)
            both = jnp.dot(low, rhs, preferred_element_type=F32)
            for kc, q in enumerate(place(ky, kx)):
                dt = softplus(both[:, kc * 128 : (kc + 1) * 128] + bias_ref[:, tile_of(q)])
                g, s = q // 8, q % 8
                dt_ref[g, pl.ds(s, ROWS, stride=8), :] = dt
                dtx_ref[g, pl.ds(s, ROWS, stride=8), :] = dt * inner_ref[:, tile_of(q)]

    def group(g, carry):
        a = [a_ref[pl.ds(pl.multiple_of(g * 128 + n * 8, 8), 8), :] for n in range(NSTATE)]

        def advance(t, hs):
            at = pl.ds(pl.multiple_of(t * 8, 8), 8)
            dt, dtx = dt_ref[g, at, :], dtx_ref[g, at, :]
            new = [
                jnp.exp2(dt * a[n]) * hs[n] + dtx * b_ref[pl.ds(t * NSTATE + n, 1), :]
                for n in range(NSTATE)
            ]
            return (*new, hs[NSTATE] + dt)

        hs = lax.fori_loop(
            0, ROWS, advance, tuple(jnp.zeros((8, 128), F32) for _ in range(NSTATE + 1)), unroll=8
        )
        for n in range(NSTATE):
            state[pl.ds(pl.multiple_of(g * 128 + n * 8, 8), 8), :] = hs[n]
        steps[pl.ds(pl.multiple_of(g * 8, 8), 8), :] = hs[NSTATE]
        return carry

    lax.fori_loop(0, GROUPS, group, 0)
    for h in range(2):
        pack(
            payload_ref.at[h], state[h * HALF : (h + 1) * HALF, :],
            steps[h * STEPPED : (h + 1) * STEPPED, :])


def pack(ref, state, steps):
    ref[:HALF, :] = state.astype(BF16)
    high = steps.astype(BF16)
    ref[HALF : HALF + STEPPED, :] = high
    ref[HALF + STEPPED :, :] = (steps - high.astype(F32)).astype(BF16)


def unpack(ref):
    value = ref[...].astype(F32)
    return value[:HALF], value[HALF : HALF + STEPPED] + value[HALF + STEPPED :]


def half_of(a_ref, h):
    return a_ref[pl.ds(pl.multiple_of(h * HALF, 16), HALF), :]


def chain(a, earlier, later):
    s = later[1].reshape(GROUPS // 2, 1, 8, 128)
    factor = jnp.exp2(a.reshape(GROUPS // 2, NSTATE, 8, 128) * s).reshape(HALF, 128)
    return factor * earlier[0] + later[0], earlier[1] + later[1]


def chip_kernel(place_ref, a_ref, own_ref, other_ref, payload_ref):
    core = place_ref[2]
    own, other = unpack(own_ref.at[core]), unpack(other_ref.at[core])
    first = tuple(jnp.where(core == 1, b, a) for a, b in zip(own, other))
    second = tuple(jnp.where(core == 1, a, b) for a, b in zip(own, other))
    pack(payload_ref, *chain(half_of(a_ref, core), first, second))


def prefix(a, stack, refs, place, total):
    count = len(refs)
    for k, ref in enumerate(refs):
        stack[k] = ref[...]

    def hop(i, carry):
        mine, run = carry
        block = unpack(stack.at[lax.rem(place - i + count, count)])
        new = chain(a, run, block)
        before = i < place
        mine = tuple(jnp.where(before, u, v) for u, v in zip(new, mine))
        return mine, new

    zero = (jnp.zeros((HALF, 128), F32), jnp.zeros((STEPPED, 128), F32))
    return lax.fori_loop(0, count if total else place, hop, (zero, zero))


def row_kernel(place_ref, a_ref, *refs):
    blocks, (payload_ref, state_ref, steps_ref, stack) = refs[:NX], refs[NX:]
    mine, run = prefix(half_of(a_ref, place_ref[2]), stack, blocks, place_ref[1], True)
    pack(payload_ref, *run)
    state_ref[...], steps_ref[...] = mine


def ahead_kernel(place_ref, a_ref, *refs):
    blocks, (state_ref, steps_ref, ahead_ref, stack) = refs[:NY], refs[NY:]
    a = half_of(a_ref, place_ref[2])
    _, run = prefix(a, stack, blocks, place_ref[0], False)
    run = chain(a, run, (state_ref[...], steps_ref[...]))
    ahead_ref[...] = run[0].astype(BF16)


def scan_kernel(place_ref, a_ref, *refs):
    (ahead_ref, other_ahead_ref, other_ref,
     dt_ref, dtx_ref, b_ref, c_ref, inner_ref, x_ref, skip_ref, gain_ref, router_ref, ids_ref,
     mixed_ref, halo_ref, sectioned_ref, state, out, moe) = refs
    core = place_ref[2]
    own = ahead_ref[...].astype(F32)
    swapped = other_ahead_ref[...].astype(F32)
    for h in range(2):
        entering = jnp.where(core == h, own, swapped)
        block = unpack(other_ref.at[h])
        after = chain(a_ref[h * HALF : (h + 1) * HALF, :], (entering, block[1]), block)[0]
        state[h * HALF : (h + 1) * HALF, :] = jnp.where(core == 1, after, entering)

    def group(g, carry):
        a = [a_ref[pl.ds(pl.multiple_of(g * 128 + n * 8, 8), 8), :] for n in range(NSTATE)]

        def advance(t, hs):
            at = pl.ds(pl.multiple_of(t * 8, 8), 8)
            dt, dtx = dt_ref[g, at, :], dtx_ref[g, at, :]
            new, parts = [], []
            for n in range(NSTATE):
                row = pl.ds(t * NSTATE + n, 1)
                h = jnp.exp2(dt * a[n]) * hs[n] + dtx * b_ref[row, :]
                new.append(h)
                part = h * c_ref[row, :]
                if n < 4:
                    parts.append(part)
                else:
                    parts[n % 4] = parts[n % 4] + part
            out[g, at, :] = (parts[0] + parts[1]) + (parts[2] + parts[3])
            return tuple(new)

        start = tuple(
            state[pl.ds(pl.multiple_of(g * 128 + n * 8, 8), 8), :] for n in range(NSTATE)
        )
        lax.fori_loop(0, ROWS, advance, start, unroll=8)
        return carry

    lax.fori_loop(0, GROUPS, group, 0)

    total = jnp.zeros((ROWS, 128), F32)
    for j in range(TILES):
        cols = slice(j * 128, (j + 1) * 128)
        scanned = out[j // 8, pl.ds(j % 8, ROWS, stride=8), :]
        mixed = (
            x_ref[:, cols].astype(F32) + (scanned + skip_ref[:, cols] * inner_ref[:, cols])
        ).astype(BF16)
        mixed_ref[:, cols] = mixed
        halo_ref[:, cols] = mixed[ROWS - HALO :]
        mixed = mixed.astype(F32)
        total = total + mixed * mixed
    scale = lax.rsqrt(jnp.sum(total, axis=1, keepdims=True) * (1.0 / WIDTH) + 1e-06)
    for j in range(TILES // 2):
        cols = slice(j * 256, (j + 1) * 256)
        moe[:, cols] = (mixed_ref[:, cols].astype(F32) * scale * gain_ref[:, cols]).astype(BF16)
    logits = lax.dot_general(
        router_ref[...], moe[...], (((1,), (1,)), ((), ())), preferred_element_type=F32
    )
    one, two = ids_ref[0:1, :], ids_ref[1:2, :]
    expert = lax.broadcasted_iota(jnp.int32, (16, ROWS), 0)
    first = jnp.sum(jnp.where(expert == one, logits, 0.0), axis=0, keepdims=True)
    second = jnp.sum(jnp.where(expert == two, logits, 0.0), axis=0, keepdims=True)
    weight_one = jax.nn.sigmoid(first - second)
    weight = jnp.where(one == 0, weight_one, jnp.where(two == 0, 1.0 - weight_one, 0.0))
    routed = jnp.where((one == 0) | (two == 0), 1.0, 0.0)
    earlier = lax.broadcasted_iota(jnp.int32, (ROWS, ROWS), 0) < lax.broadcasted_iota(
        jnp.int32, (ROWS, ROWS), 1
    )
    ahead_of = jnp.dot(
        jnp.broadcast_to(routed, (8, ROWS)), jnp.where(earlier, 1.0, 0.0), preferred_element_type=F32
    )
    slot = lax.broadcasted_iota(jnp.int32, (SLOTS, ROWS), 0).astype(F32)
    chosen = jnp.where((ahead_of == slot) & (routed > 0.0), 1.0, 0.0)
    weights = chosen * weight
    high = weights.astype(BF16).astype(F32)
    slots = jnp.concatenate([high, weights - high], 0).astype(BF16)
    mixed_ref[:16, WIDTH:] = slots
    mixed_ref[16:, WIDTH:] = jnp.zeros((ROWS - 16, EXTRA), BF16)
    halo_ref[:, WIDTH:] = slots
    sectioned_ref[...] = jnp.dot(
        chosen.astype(BF16), moe[...], preferred_element_type=F32
    ).astype(BF16)


def final_kernel(x_ref, out_ref, y_ref):
    slots = x_ref[:16, WIDTH:]
    for j in range(WIDTH // 512):
        cols = slice(j * 512, (j + 1) * 512)
        y_ref[:, cols] = (x_ref[:, cols].astype(F32) + slot_rows(slots, out_ref, cols)).astype(BF16)


def expert_kernel(*refs):
    pieces, refs = refs[: NC * NY], refs[NC * NY :]
    gate_ref, up_ref, down_ref, own_ref, other_ref, xs = refs
    rows = NX * SLOTS
    for k, piece in enumerate(pieces):
        xs[k * rows : (k + 1) * rows, :] = piece[...]
    gate = jnp.dot(xs[...], gate_ref[...], preferred_element_type=F32)
    up = jnp.dot(xs[...], up_ref[...], preferred_element_type=F32)
    hidden = (gate * jax.nn.sigmoid(gate) * up).astype(BF16)
    half = NY * rows
    for j in range(WIDTH // 512):
        cols = slice(j * 512, (j + 1) * 512)
        terms = jnp.dot(hidden, down_ref[:, cols], preferred_element_type=F32).astype(BF16)
        own_ref[:, cols] = terms[:half]
        other_ref[:, cols] = terms[half:]


def sum_kernel(count, *refs):
    ins, outs = refs[:count], refs[count:]
    rows = outs[0].shape[0]
    for j in range(WIDTH // 512):
        cols = slice(j * 512, (j + 1) * 512)
        total = ins[0][:, cols].astype(F32)
        for ref in ins[1:]:
            total = total + ref[:, cols].astype(F32)
        for k, ref in enumerate(outs):
            ref[:, cols] = total[k * rows : (k + 1) * rows].astype(BF16)


def index(y, x, c):
    return (y % NY) * NX * NC + (x % NX) * NC + c % NC


def shifted(block, dy, dx, dc):
    route = [
        (index(y, x, c), index(y + dy, x + dx, c + dc))
        for y in range(NY)
        for x in range(NX)
        for c in range(NC)
    ]
    return lax.ppermute(block, "seq", route)


def onward(block, sections, distance):
    route = [
        (s * NQ + q, (s + 1) % sections * NQ + q + distance)
        for s in range(sections)
        for q in range(NQ)
        if q + distance < NQ
    ]
    return lax.ppermute(block, ("section", "seq"), route)


def along_x(block):
    return [block] + [shifted(block, 0, k, 0) for k in range(1, NX)]


def along_y(block):
    return [block] + [shifted(block, k, 0, 0) for k in range(1, NY)]


def along_core(blocks):
    return list(blocks) + [shifted(block, 0, 0, 1) for block in blocks]


def body(
    input_in_transit,
    mixer_norm_gain,
    convolution_weight,
    convolution_bias,
    input_projection,
    step_size_projection,
    step_size_bias,
    log_decay_rates,
    mixer_skip_weight,
    expert_norm_gain,
    router,
    gate_weight,
    up_weight,
    down_weight,
    expert_index_table,
):
    sections = lax.axis_size("section")
    q = lax.axis_index("seq")
    y, x, c = q // (NX * NC), q // NC % NX, q % NC
    place = jnp.stack([y, x, c]).astype(jnp.int32)
    sds = jax.ShapeDtypeStruct

    rates = (-LOG2E) * jnp.exp(log_decay_rates[0])
    rates = rates.reshape(GROUPS, 8, 128, NSTATE).transpose(0, 3, 1, 2)
    rates = rates.reshape(GROUPS * NSTATE * 8, 128)
    router_t = router[0].T
    ids = expert_index_table[:, 0].transpose(0, 2, 1)

    kc, ky, kx = jnp.meshgrid(jnp.arange(NC), jnp.arange(NY), jnp.arange(NX), indexing="ij")
    order = (y - ky) % NY * (NX * NC) + (x - kx) % NX * NC + (c + kc) % NC
    order = order.reshape(NQ).astype(jnp.int32)

    present = input_in_transit[0]
    behind = lax.ppermute(present[ROWS - HALO :], "seq", [(i, i + 1) for i in range(NQ - 1)])
    gains = [mixer_norm_gain, convolution_weight[0], convolution_bias]
    inner_shape = sds((ROWS, WIDTH), F32)
    rows = pltpu.VMEM((HALO + ROWS, WIDTH), F32)

    w = jnp.stack(along_x(input_projection[0].T))
    wdt = jnp.stack(along_y(step_size_projection[0]))
    (inner,) = call(
        functools.partial(pre_kernel, True), [present, behind, *gains], [inner_shape], [rows], name="pre"
    )
    w, wdt, inner, rates, order, place, router_t, ids = lax.optimization_barrier(
        (w, wdt, inner, rates, order, place, router_t, ids)
    )
    w, wdt = along_core(along_y(w)), along_core(along_x(wdt))

    handed = None
    for step in range(STEPS):
        if step:
            inner, present = call(
                functools.partial(pre_kernel, False), [*handed, *gains],
                [inner_shape, sds((ROWS, WIDTH), BF16)], [rows], name="pre_next")
        wide = sds((GROUPS, ROWS * 8, 128), F32)
        tall = sds((ROWS * NSTATE, 128), F32)
        packed = sds((PAYLOAD, 128), BF16)
        halves = sds((2, PAYLOAD, 128), BF16)
        states = pltpu.VMEM((GROUPS * NSTATE * 8, 128), F32)
        stack = pltpu.VMEM((NX, PAYLOAD, 128), BF16)
        dt, dtx, b, c_out, payload = call(
            main_kernel, [order, inner, step_size_bias, rates, *w, *wdt],
            [wide, wide, tall, tall, halves], [states, pltpu.VMEM((TILES, 128), F32)], n_smem=1,
            name="project_and_end", mib=24)
        other = shifted(payload, 0, 0, 1)
        (chip,) = call(chip_kernel, [place, rates, payload, other], [packed], n_smem=1, name="chip", mib=8)
        row, row_state, row_steps = call(
            row_kernel, [place, rates, *along_x(chip)],
            [packed, sds((HALF, 128), F32), sds((STEPPED, 128), F32)], [stack], n_smem=1,
            name="row", mib=8)
        (ahead,) = call(
            ahead_kernel, [place, rates, *along_y(row), row_state, row_steps],
            [sds((HALF, 128), BF16)], [stack], n_smem=1, name="ahead", mib=8)
        mixed, halo, sectioned = call(
            scan_kernel,
            [place, rates, ahead, shifted(ahead, 0, 0, 1), other, dt, dtx, b, c_out, inner, present,
             mixer_skip_weight, expert_norm_gain, router_t, ids[step]],
            [sds((ROWS, WIDTH + EXTRA), BF16), sds((HALO, WIDTH + EXTRA), BF16), sds((SLOTS, WIDTH), BF16)],
            [states, pltpu.VMEM((GROUPS, ROWS * 8, 128), F32), pltpu.VMEM((ROWS, WIDTH), BF16)],
            n_smem=1, name="scan", mib=24)
        last = step + 1 == STEPS
        if not last:
            handed = [onward(mixed, sections, 0), onward(halo, sections, 1)]
        gathered = jnp.concatenate(along_x(sectioned), 0)
        gathered = along_core(along_y(gathered))
        half = sds((ROWS, WIDTH), BF16)
        own, others = call(
            expert_kernel, [*gathered, gate_weight[0], up_weight[0], down_weight[0]], [half, half],
            [pltpu.VMEM((NQ * SLOTS, WIDTH), BF16)], name="expert", mib=32)
        own = call(
            functools.partial(sum_kernel, NC), [own, shifted(others, 0, 0, 1)],
            [sds((NX * SLOTS, WIDTH), BF16)] * NY, name="sum_core", mib=8)
        own = call(
            functools.partial(sum_kernel, NY), [own[0]] + [shifted(own[k], -k, 0, 0) for k in range(1, NY)],
            [sds((SLOTS, WIDTH), BF16)] * NX, name="sum_y", mib=8)
        (expert_out,) = call(
            functools.partial(sum_kernel, NX), [own[0]] + [shifted(own[k], 0, -k, 0) for k in range(1, NX)],
            [sds((SLOTS, WIDTH), BF16)], name="sum_x", mib=8)
        if last:
            (produced,) = call(
                final_kernel, [mixed, expert_out], [sds((ROWS, WIDTH), BF16)], name="final", mib=8
            )
        else:
            handed += [onward(expert_out, sections, 0), onward(expert_out, sections, 1)]
    return produced[None]


def solution(mesh):
    return jax.shard_map(
        body,
        mesh=mesh,
        in_specs=(
            P("section", "seq", None),
            P("section", None),
            P("section", None, None),
            P("section", None),
            P("section", "seq", None),
            P("section", None, "seq"),
            P("section", None),
            P("section", None, None),
            P("section", None),
            P("section", None),
            P("section", None, None),
            P("section", None, "seq"),
            P("section", None, "seq"),
            P("section", "seq", None),
            P(None, "section", "seq", None),
        ),
        out_specs=P("section", "seq", None),
        check_vma=False,
    )
```

```python
import functools

import jax
import jax.numpy as jnp
from jax import lax
from jax.experimental import pallas as pl
from jax.experimental.pallas import tpu as pltpu
from jax.sharding import PartitionSpec as P

STEPS = 2
ROWS = 128
WIDTH = 4096
NSTATE = 16
RANK = 256
SLOTS = 8
TILES = WIDTH // 128
GROUPS = 4
HALO = 16
EXTRA = 128
NY, NX, NC = 4, 4, 2
NQ = NY * NX * NC
LOG2E = 1.4426950408889634
HALF = GROUPS // 2 * NSTATE * 8
STEPPED = TILES // 2
PAYLOAD = HALF + 2 * STEPPED
F32, BF16 = jnp.float32, jnp.bfloat16

VMEM = pl.BlockSpec(memory_space=pltpu.VMEM)
SMEM = pl.BlockSpec(memory_space=pltpu.SMEM)


def call(kernel, ins, outs, scratch=(), n_smem=0, flops=0, name=None, mib=16):
    moved = sum(v.size * v.dtype.itemsize for v in ins) + sum(
        o.size * o.dtype.itemsize for o in outs
    )
    return pl.pallas_call(
        kernel,
        out_shape=outs,
        in_specs=[SMEM] * n_smem + [VMEM] * (len(ins) - n_smem),
        out_specs=[VMEM] * len(outs),
        scratch_shapes=list(scratch),
        compiler_params=pltpu.CompilerParams(vmem_limit_bytes=mib * 1024 * 1024),
        cost_estimate=pl.CostEstimate(flops=flops, bytes_accessed=moved, transcendentals=0),
        name=name,
    )(*ins)


def tile_of(j):
    return pl.ds(pl.multiple_of(j * 128, 128), 128)


def slot_rows(slots, out_ref, cols):
    out = out_ref[:, cols].astype(F32)
    out = jnp.concatenate([out, out], 0).astype(BF16)
    return lax.dot_general(slots, out, (((0,), (0,)), ((), ())), preferred_element_type=F32)


def pre_kernel(fresh, *refs):
    if fresh:
        x_ref, halo_ref, gain_ref, taps_ref, bias_ref, inner_ref, rows = refs
    else:
        (x_ref, halo_ref, out_ref, halo_out_ref,
         gain_ref, taps_ref, bias_ref, inner_ref, x_out_ref, rows) = refs
        slots, halo_slots = x_ref[:16, WIDTH:], halo_ref[:, WIDTH:]
    chunk = 512
    total = jnp.zeros((HALO + ROWS, 128), F32)
    for j in range(WIDTH // chunk):
        cols = slice(j * chunk, (j + 1) * chunk)
        own = x_ref[:, cols].astype(F32)
        behind = halo_ref[:, cols].astype(F32)
        if not fresh:
            own = (own + slot_rows(slots, out_ref, cols)).astype(BF16)
            x_out_ref[:, cols] = own
            own = own.astype(F32)
            add = slot_rows(halo_slots, halo_out_ref, cols)
            behind = (behind + add[ROWS - HALO :]).astype(BF16).astype(F32)
        both = jnp.concatenate([behind, own], 0)
        rows[:, cols] = both
        square = both * both
        for i in range(chunk // 128):
            total = total + square[:, i * 128 : (i + 1) * 128]
    scale = lax.rsqrt(jnp.sum(total, axis=1, keepdims=True) * (1.0 / WIDTH) + 1e-06)
    chunk = 256
    for j in range(WIDTH // chunk):
        cols = slice(j * chunk, (j + 1) * chunk)
        normed = (rows[:, cols] * scale * gain_ref[:, cols]).astype(BF16).astype(F32)
        rows[:, cols] = normed
        acc = bias_ref[:, cols]
        for k in range(4):
            first = HALO - 3 + k
            acc = acc + taps_ref[k : k + 1, cols] * rows[first : first + ROWS, cols]
        inner_ref[:, cols] = acc * jax.nn.sigmoid(acc)


def softplus(z):
    e = jnp.exp(-jnp.abs(z))
    small = e * (1.0 - e * (0.5 - e * (1.0 / 3.0)))
    return jnp.maximum(z, 0.0) + jnp.where(e < 0.005, small, jnp.log(1.0 + e))


def main_kernel(order_ref, inner_ref, bias_ref, a_ref, *refs):
    w, wdt = refs[: NC * NY], refs[NC * NY : NC * (NY + NX)]
    dt_ref, dtx_ref, b_ref, c_ref, payload_ref, state, steps = refs[NC * (NY + NX) :]

    def place(ky, kx):
        return [order_ref[(kc * NY + ky) * NX + kx] for kc in range(NC)]

    projected = jnp.zeros((ROWS, RANK + 2 * NSTATE), F32)
    for ky in range(NY):
        for kx in range(NX):
            lhs = [inner_ref[:, tile_of(q)].astype(BF16) for q in place(ky, kx)]
            rhs = [w[kc * NY + ky][kx] for kc in range(NC)]
            projected = projected + lax.dot_general(
                jnp.concatenate(lhs, 1), jnp.concatenate(rhs, 1), (((1,), (1,)), ((), ())),
                preferred_element_type=F32)
    low = projected[:, :RANK].astype(BF16)
    for n in range(NSTATE):
        for ref, at in ((b_ref, RANK), (c_ref, RANK + NSTATE)):
            column = projected[:, at + n : at + n + 1]
            ref[pl.ds(n, ROWS, stride=NSTATE), :] = jnp.broadcast_to(column, (ROWS, 128))

    for kx in range(NX):
        for ky in range(NY):
            rhs = jnp.concatenate([wdt[kc * NX + kx][ky] for kc in range(NC)], 1)
            both = jnp.dot(low, rhs, preferred_element_type=F32)
            for kc, q in enumerate(place(ky, kx)):
                dt = softplus(both[:, kc * 128 : (kc + 1) * 128] + bias_ref[:, tile_of(q)])
                g, s = q // 8, q % 8
                dt_ref[g, pl.ds(s, ROWS, stride=8), :] = dt
                dtx_ref[g, pl.ds(s, ROWS, stride=8), :] = dt * inner_ref[:, tile_of(q)]

    def group(g, carry):
        a = [a_ref[pl.ds(pl.multiple_of(g * 128 + n * 8, 8), 8), :] for n in range(NSTATE)]

        def advance(t, hs):
            at = pl.ds(pl.multiple_of(t * 8, 8), 8)
            dt, dtx = dt_ref[g, at, :], dtx_ref[g, at, :]
            new = [
                jnp.exp2(dt * a[n]) * hs[n] + dtx * b_ref[pl.ds(t * NSTATE + n, 1), :]
                for n in range(NSTATE)
            ]
            return (*new, hs[NSTATE] + dt)

        hs = lax.fori_loop(
            0, ROWS, advance, tuple(jnp.zeros((8, 128), F32) for _ in range(NSTATE + 1)), unroll=8
        )
        for n in range(NSTATE):
            state[pl.ds(pl.multiple_of(g * 128 + n * 8, 8), 8), :] = hs[n]
        steps[pl.ds(pl.multiple_of(g * 8, 8), 8), :] = hs[NSTATE]
        return carry

    lax.fori_loop(0, GROUPS, group, 0)
    for h in range(2):
        pack(
            payload_ref.at[h], state[h * HALF : (h + 1) * HALF, :],
            steps[h * STEPPED : (h + 1) * STEPPED, :])


def pack(ref, state, steps):
    ref[:HALF, :] = state.astype(BF16)
    high = steps.astype(BF16)
    ref[HALF : HALF + STEPPED, :] = high
    ref[HALF + STEPPED :, :] = (steps - high.astype(F32)).astype(BF16)


def unpack(ref):
    value = ref[...].astype(F32)
    return value[:HALF], value[HALF : HALF + STEPPED] + value[HALF + STEPPED :]


def half_of(a_ref, h):
    return a_ref[pl.ds(pl.multiple_of(h * HALF, 16), HALF), :]


def chain(a, earlier, later):
    s = later[1].reshape(GROUPS // 2, 1, 8, 128)
    factor = jnp.exp2(a.reshape(GROUPS // 2, NSTATE, 8, 128) * s).reshape(HALF, 128)
    return factor * earlier[0] + later[0], earlier[1] + later[1]


def chip_kernel(place_ref, a_ref, own_ref, other_ref, payload_ref):
    core = place_ref[2]
    own, other = unpack(own_ref.at[core]), unpack(other_ref.at[core])
    first = tuple(jnp.where(core == 1, b, a) for a, b in zip(own, other))
    second = tuple(jnp.where(core == 1, a, b) for a, b in zip(own, other))
    pack(payload_ref, *chain(half_of(a_ref, core), first, second))


def prefix(a, stack, refs, place, total):
    count = len(refs)
    for k, ref in enumerate(refs):
        stack[k] = ref[...]

    def hop(i, carry):
        mine, run = carry
        block = unpack(stack.at[lax.rem(place - i + count, count)])
        new = chain(a, run, block)
        before = i < place
        mine = tuple(jnp.where(before, u, v) for u, v in zip(new, mine))
        return mine, new

    zero = (jnp.zeros((HALF, 128), F32), jnp.zeros((STEPPED, 128), F32))
    return lax.fori_loop(0, count if total else place, hop, (zero, zero))


def row_kernel(place_ref, a_ref, *refs):
    blocks, (payload_ref, state_ref, steps_ref, stack) = refs[:NX], refs[NX:]
    mine, run = prefix(half_of(a_ref, place_ref[2]), stack, blocks, place_ref[1], True)
    pack(payload_ref, *run)
    state_ref[...], steps_ref[...] = mine


def ahead_kernel(place_ref, a_ref, *refs):
    blocks, (state_ref, steps_ref, ahead_ref, stack) = refs[:NY], refs[NY:]
    a = half_of(a_ref, place_ref[2])
    _, run = prefix(a, stack, blocks, place_ref[0], False)
    run = chain(a, run, (state_ref[...], steps_ref[...]))
    ahead_ref[...] = run[0].astype(BF16)


def scan_kernel(place_ref, a_ref, *refs):
    (ahead_ref, other_ahead_ref, other_ref,
     dt_ref, dtx_ref, b_ref, c_ref, inner_ref, x_ref, skip_ref, gain_ref, router_ref, ids_ref,
     mixed_ref, halo_ref, sectioned_ref, state, out, moe) = refs
    core = place_ref[2]
    own = ahead_ref[...].astype(F32)
    swapped = other_ahead_ref[...].astype(F32)
    for h in range(2):
        entering = jnp.where(core == h, own, swapped)
        block = unpack(other_ref.at[h])
        after = chain(a_ref[h * HALF : (h + 1) * HALF, :], (entering, block[1]), block)[0]
        state[h * HALF : (h + 1) * HALF, :] = jnp.where(core == 1, after, entering)

    def group(g, carry):
        a = [a_ref[pl.ds(pl.multiple_of(g * 128 + n * 8, 8), 8), :] for n in range(NSTATE)]

        def advance(t, hs):
            at = pl.ds(pl.multiple_of(t * 8, 8), 8)
            dt, dtx = dt_ref[g, at, :], dtx_ref[g, at, :]
            new, parts = [], []
            for n in range(NSTATE):
                row = pl.ds(t * NSTATE + n, 1)
                h = jnp.exp2(dt * a[n]) * hs[n] + dtx * b_ref[row, :]
                new.append(h)
                part = h * c_ref[row, :]
                if n < 4:
                    parts.append(part)
                else:
                    parts[n % 4] = parts[n % 4] + part
            out[g, at, :] = (parts[0] + parts[1]) + (parts[2] + parts[3])
            return tuple(new)

        start = tuple(
            state[pl.ds(pl.multiple_of(g * 128 + n * 8, 8), 8), :] for n in range(NSTATE)
        )
        lax.fori_loop(0, ROWS, advance, start, unroll=8)
        return carry

    lax.fori_loop(0, GROUPS, group, 0)

    total = jnp.zeros((ROWS, 128), F32)
    for j in range(TILES):
        cols = slice(j * 128, (j + 1) * 128)
        scanned = out[j // 8, pl.ds(j % 8, ROWS, stride=8), :]
        mixed = (
            x_ref[:, cols].astype(F32) + (scanned + skip_ref[:, cols] * inner_ref[:, cols])
        ).astype(BF16)
        mixed_ref[:, cols] = mixed
        halo_ref[:, cols] = mixed[ROWS - HALO :]
        mixed = mixed.astype(F32)
        total = total + mixed * mixed
    scale = lax.rsqrt(jnp.sum(total, axis=1, keepdims=True) * (1.0 / WIDTH) + 1e-06)
    for j in range(TILES // 2):
        cols = slice(j * 256, (j + 1) * 256)
        moe[:, cols] = (mixed_ref[:, cols].astype(F32) * scale * gain_ref[:, cols]).astype(BF16)
    logits = lax.dot_general(
        router_ref[...], moe[...], (((1,), (1,)), ((), ())), preferred_element_type=F32
    )
    one, two = ids_ref[0:1, :], ids_ref[1:2, :]
    expert = lax.broadcasted_iota(jnp.int32, (16, ROWS), 0)
    first = jnp.sum(jnp.where(expert == one, logits, 0.0), axis=0, keepdims=True)
    second = jnp.sum(jnp.where(expert == two, logits, 0.0), axis=0, keepdims=True)
    weight_one = jax.nn.sigmoid(first - second)
    weight = jnp.where(one == 0, weight_one, jnp.where(two == 0, 1.0 - weight_one, 0.0))
    routed = jnp.where((one == 0) | (two == 0), 1.0, 0.0)
    earlier = lax.broadcasted_iota(jnp.int32, (ROWS, ROWS), 0) < lax.broadcasted_iota(
        jnp.int32, (ROWS, ROWS), 1
    )
    ahead_of = jnp.dot(
        jnp.broadcast_to(routed, (8, ROWS)), jnp.where(earlier, 1.0, 0.0), preferred_element_type=F32
    )
    slot = lax.broadcasted_iota(jnp.int32, (SLOTS, ROWS), 0).astype(F32)
    chosen = jnp.where((ahead_of == slot) & (routed > 0.0), 1.0, 0.0)
    weights = chosen * weight
    high = weights.astype(BF16).astype(F32)
    slots = jnp.concatenate([high, weights - high], 0).astype(BF16)
    mixed_ref[:16, WIDTH:] = slots
    mixed_ref[16:, WIDTH:] = jnp.zeros((ROWS - 16, EXTRA), BF16)
    halo_ref[:, WIDTH:] = slots
    sectioned_ref[...] = jnp.dot(
        chosen.astype(BF16), moe[...], preferred_element_type=F32
    ).astype(BF16)


def final_kernel(x_ref, out_ref, y_ref):
    slots = x_ref[:16, WIDTH:]
    for j in range(WIDTH // 512):
        cols = slice(j * 512, (j + 1) * 512)
        y_ref[:, cols] = (x_ref[:, cols].astype(F32) + slot_rows(slots, out_ref, cols)).astype(BF16)


def expert_kernel(*refs):
    pieces, refs = refs[: NC * NY], refs[NC * NY :]
    gate_ref, up_ref, down_ref, own_ref, other_ref, xs = refs
    rows = NX * SLOTS
    for k, piece in enumerate(pieces):
        xs[k * rows : (k + 1) * rows, :] = piece[...]
    gate = jnp.dot(xs[...], gate_ref[...], preferred_element_type=F32)
    up = jnp.dot(xs[...], up_ref[...], preferred_element_type=F32)
    hidden = (gate * jax.nn.sigmoid(gate) * up).astype(BF16)
    half = NY * rows
    for j in range(WIDTH // 512):
        cols = slice(j * 512, (j + 1) * 512)
        terms = jnp.dot(hidden, down_ref[:, cols], preferred_element_type=F32).astype(BF16)
        own_ref[:, cols] = terms[:half]
        other_ref[:, cols] = terms[half:]


def sum_kernel(count, *refs):
    ins, outs = refs[:count], refs[count:]
    rows = outs[0].shape[0]
    for j in range(WIDTH // 512):
        cols = slice(j * 512, (j + 1) * 512)
        total = ins[0][:, cols].astype(F32)
        for ref in ins[1:]:
            total = total + ref[:, cols].astype(F32)
        for k, ref in enumerate(outs):
            ref[:, cols] = total[k * rows : (k + 1) * rows].astype(BF16)


def index(y, x, c):
    return (y % NY) * NX * NC + (x % NX) * NC + c % NC


def shifted(block, dy, dx, dc):
    route = [
        (index(y, x, c), index(y + dy, x + dx, c + dc))
        for y in range(NY)
        for x in range(NX)
        for c in range(NC)
    ]
    return lax.ppermute(block, "seq", route)


def onward(block, sections, distance):
    route = [
        (s * NQ + q, (s + 1) % sections * NQ + q + distance)
        for s in range(sections)
        for q in range(NQ)
        if q + distance < NQ
    ]
    return lax.ppermute(block, ("section", "seq"), route)


def crossed(block, first, second):
    route = []
    for y in range(NY):
        for x in range(NX):
            route.append((index(y, x, 0), index(y + second, x + first, 0)))
            route.append((index(y, x, 1), index(y + first, x + second, 1)))
    return lax.ppermute(block, "seq", route)


def along_x(block):
    return [block] + [shifted(block, 0, k, 0) for k in range(1, NX)]


def along_y(block):
    return [block] + [shifted(block, k, 0, 0) for k in range(1, NY)]


def along_core(blocks):
    return list(blocks) + [shifted(block, 0, 0, 1) for block in blocks]


def body(
    input_in_transit,
    mixer_norm_gain,
    convolution_weight,
    convolution_bias,
    input_projection,
    step_size_projection,
    step_size_bias,
    log_decay_rates,
    mixer_skip_weight,
    expert_norm_gain,
    router,
    gate_weight,
    up_weight,
    down_weight,
    expert_index_table,
):
    sections = lax.axis_size("section")
    q = lax.axis_index("seq")
    y, x, c = q // (NX * NC), q // NC % NX, q % NC
    place = jnp.stack([y, x, c]).astype(jnp.int32)
    sds = jax.ShapeDtypeStruct

    rates = (-LOG2E) * jnp.exp(log_decay_rates[0])
    rates = rates.reshape(GROUPS, 8, 128, NSTATE).transpose(0, 3, 1, 2)
    rates = rates.reshape(GROUPS * NSTATE * 8, 128)
    router_t = router[0].T
    ids = expert_index_table[:, 0].transpose(0, 2, 1)

    kc, ky, kx = jnp.meshgrid(jnp.arange(NC), jnp.arange(NY), jnp.arange(NX), indexing="ij")
    order = (y - ky) % NY * (NX * NC) + (x - kx) % NX * NC + (c + kc) % NC
    order = order.reshape(NQ).astype(jnp.int32)

    present = input_in_transit[0]
    behind = lax.ppermute(present[ROWS - HALO :], "seq", [(i, i + 1) for i in range(NQ - 1)])
    gains = [mixer_norm_gain, convolution_weight[0], convolution_bias]
    inner_shape = sds((ROWS, WIDTH), F32)
    rows = pltpu.VMEM((HALO + ROWS, WIDTH), F32)

    w = jnp.stack(along_x(input_projection[0].T))
    wdt = jnp.stack(along_y(step_size_projection[0]))
    (inner,) = call(
        functools.partial(pre_kernel, True), [present, behind, *gains], [inner_shape], [rows], name="pre"
    )
    w, wdt, inner, rates, order, place, router_t, ids = lax.optimization_barrier(
        (w, wdt, inner, rates, order, place, router_t, ids)
    )
    w, wdt = along_core(along_y(w)), along_core(along_x(wdt))

    handed = None
    for step in range(STEPS):
        if step:
            inner, present = call(
                functools.partial(pre_kernel, False), [*handed, *gains],
                [inner_shape, sds((ROWS, WIDTH), BF16)], [rows], name="pre_next")
        wide = sds((GROUPS, ROWS * 8, 128), F32)
        tall = sds((ROWS * NSTATE, 128), F32)
        packed = sds((PAYLOAD, 128), BF16)
        halves = sds((2, PAYLOAD, 128), BF16)
        states = pltpu.VMEM((GROUPS * NSTATE * 8, 128), F32)
        stack = pltpu.VMEM((NX, PAYLOAD, 128), BF16)
        dt, dtx, b, c_out, payload = call(
            main_kernel, [order, inner, step_size_bias, rates, *w, *wdt],
            [wide, wide, tall, tall, halves], [states, pltpu.VMEM((TILES, 128), F32)], n_smem=1,
            name="project_and_end", mib=24)
        other = shifted(payload, 0, 0, 1)
        (chip,) = call(chip_kernel, [place, rates, payload, other], [packed], n_smem=1, name="chip", mib=8)
        chips, row_state, row_steps = call(
            row_kernel, [place, rates, *along_x(chip)],
            [packed, sds((HALF, 128), F32), sds((STEPPED, 128), F32)], [stack], n_smem=1,
            name="row", mib=8)
        (ahead,) = call(
            ahead_kernel, [place, rates, *along_y(chips), row_state, row_steps],
            [sds((HALF, 128), BF16)], [stack], n_smem=1, name="ahead", mib=8)
        mixed, halo, sectioned = call(
            scan_kernel,
            [place, rates, ahead, shifted(ahead, 0, 0, 1), other, dt, dtx, b, c_out, inner, present,
             mixer_skip_weight, expert_norm_gain, router_t, ids[step]],
            [sds((ROWS, WIDTH + EXTRA), BF16), sds((HALO, WIDTH + EXTRA), BF16), sds((SLOTS, WIDTH), BF16)],
            [states, pltpu.VMEM((GROUPS, ROWS * 8, 128), F32), pltpu.VMEM((ROWS, WIDTH), BF16)],
            n_smem=1, name="scan", mib=24)
        last = step + 1 == STEPS
        if not last:
            handed = [onward(mixed, sections, 0), onward(halo, sections, 1)]
        gathered = [sectioned] + [crossed(sectioned, k, 0) for k in range(1, NX)]
        gathered = jnp.concatenate(gathered, 0)
        gathered = [gathered] + [crossed(gathered, 0, k) for k in range(1, NY)]
        gathered = along_core(gathered)
        half = sds((ROWS, WIDTH), BF16)
        own, others = call(
            expert_kernel, [*gathered, gate_weight[0], up_weight[0], down_weight[0]], [half, half],
            [pltpu.VMEM((NQ * SLOTS, WIDTH), BF16)], name="expert", mib=32)
        own = call(
            functools.partial(sum_kernel, NC), [own, shifted(others, 0, 0, 1)],
            [sds((NX * SLOTS, WIDTH), BF16)] * NY, name="sum_core", mib=8)
        own = call(
            functools.partial(sum_kernel, NY), [own[0]] + [crossed(own[k], 0, -k) for k in range(1, NY)],
            [sds((SLOTS, WIDTH), BF16)] * NX, name="sum_second", mib=8)
        (expert_out,) = call(
            functools.partial(sum_kernel, NX), [own[0]] + [crossed(own[k], -k, 0) for k in range(1, NX)],
            [sds((SLOTS, WIDTH), BF16)], name="sum_first", mib=8)
        if last:
            (produced,) = call(
                final_kernel, [mixed, expert_out], [sds((ROWS, WIDTH), BF16)], name="final", mib=8
            )
        else:
            handed += [onward(expert_out, sections, 0), onward(expert_out, sections, 1)]
    return produced[None]


def solution(mesh):
    return jax.shard_map(
        body,
        mesh=mesh,
        in_specs=(
            P("section", "seq", None),
            P("section", None),
            P("section", None, None),
            P("section", None),
            P("section", "seq", None),
            P("section", None, "seq"),
            P("section", None),
            P("section", None, None),
            P("section", None),
            P("section", None),
            P("section", None, None),
            P("section", None, "seq"),
            P("section", None, "seq"),
            P("section", "seq", None),
            P(None, "section", "seq", None),
        ),
        out_specs=P("section", "seq", None),
        check_vma=False,
    )
```

```python
import functools

import jax
import jax.numpy as jnp
from jax import lax
from jax.experimental import pallas as pl
from jax.experimental.pallas import tpu as pltpu
from jax.sharding import PartitionSpec as P

STEPS = 2
ROWS = 128
WIDTH = 4096
NSTATE = 16
RANK = 256
SLOTS = 8
TILES = WIDTH // 128
GROUPS = 4
HALO = 16
EXTRA = 128
NY, NX, NC = 4, 4, 2
NQ = NY * NX * NC
LOG2E = 1.4426950408889634
HALF = GROUPS // 2 * NSTATE * 8
STEPPED = TILES // 2
PAYLOAD = HALF + 2 * STEPPED
F32, BF16 = jnp.float32, jnp.bfloat16

VMEM = pl.BlockSpec(memory_space=pltpu.VMEM)
SMEM = pl.BlockSpec(memory_space=pltpu.SMEM)


def call(kernel, ins, outs, scratch=(), n_smem=0, flops=0, name=None, mib=16):
    moved = sum(v.size * v.dtype.itemsize for v in ins) + sum(
        o.size * o.dtype.itemsize for o in outs
    )
    return pl.pallas_call(
        kernel,
        out_shape=outs,
        in_specs=[SMEM] * n_smem + [VMEM] * (len(ins) - n_smem),
        out_specs=[VMEM] * len(outs),
        scratch_shapes=list(scratch),
        compiler_params=pltpu.CompilerParams(vmem_limit_bytes=mib * 1024 * 1024),
        cost_estimate=pl.CostEstimate(flops=flops, bytes_accessed=moved, transcendentals=0),
        name=name,
    )(*ins)


def tile_of(j):
    return pl.ds(pl.multiple_of(j * 128, 128), 128)


def slot_rows(slots, out_ref, cols):
    out = out_ref[:, cols].astype(F32)
    out = jnp.concatenate([out, out], 0).astype(BF16)
    return lax.dot_general(slots, out, (((0,), (0,)), ((), ())), preferred_element_type=F32)


def pre_kernel(fresh, *refs):
    if fresh:
        x_ref, halo_ref, gain_ref, taps_ref, bias_ref, inner_ref, rows = refs
    else:
        (x_ref, halo_ref, out_ref, halo_out_ref,
         gain_ref, taps_ref, bias_ref, inner_ref, x_out_ref, rows) = refs
        slots, halo_slots = x_ref[:16, WIDTH:], halo_ref[:, WIDTH:]
    chunk = 512
    total = jnp.zeros((HALO + ROWS, 128), F32)
    for j in range(WIDTH // chunk):
        cols = slice(j * chunk, (j + 1) * chunk)
        own = x_ref[:, cols].astype(F32)
        behind = halo_ref[:, cols].astype(F32)
        if not fresh:
            own = (own + slot_rows(slots, out_ref, cols)).astype(BF16)
            x_out_ref[:, cols] = own
            own = own.astype(F32)
            add = slot_rows(halo_slots, halo_out_ref, cols)
            behind = (behind + add[ROWS - HALO :]).astype(BF16).astype(F32)
        both = jnp.concatenate([behind, own], 0)
        rows[:, cols] = both
        square = both * both
        for i in range(chunk // 128):
            total = total + square[:, i * 128 : (i + 1) * 128]
    scale = lax.rsqrt(jnp.sum(total, axis=1, keepdims=True) * (1.0 / WIDTH) + 1e-06)
    chunk = 256
    for j in range(WIDTH // chunk):
        cols = slice(j * chunk, (j + 1) * chunk)
        normed = (rows[:, cols] * scale * gain_ref[:, cols]).astype(BF16).astype(F32)
        rows[:, cols] = normed
        acc = bias_ref[:, cols]
        for k in range(4):
            first = HALO - 3 + k
            acc = acc + taps_ref[k : k + 1, cols] * rows[first : first + ROWS, cols]
        inner_ref[:, cols] = acc * jax.nn.sigmoid(acc)


def softplus(z):
    e = jnp.exp(-jnp.abs(z))
    small = e * (1.0 - e * (0.5 - e * (1.0 / 3.0)))
    return jnp.maximum(z, 0.0) + jnp.where(e < 0.005, small, jnp.log(1.0 + e))


def main_kernel(order_ref, inner_ref, bias_ref, a_ref, *refs):
    w, wdt = refs[: NC * NY], refs[NC * NY : NC * (NY + NX)]
    dt_ref, dtx_ref, b_ref, c_ref, payload_ref, state, steps = refs[NC * (NY + NX) :]

    def place(ky, kx):
        return [order_ref[(kc * NY + ky) * NX + kx] for kc in range(NC)]

    projected = jnp.zeros((ROWS, RANK + 2 * NSTATE), F32)
    for ky in range(NY):
        for kx in range(NX):
            lhs = [inner_ref[:, tile_of(q)].astype(BF16) for q in place(ky, kx)]
            rhs = [w[kc * NY + ky][kx] for kc in range(NC)]
            projected = projected + lax.dot_general(
                jnp.concatenate(lhs, 1), jnp.concatenate(rhs, 1), (((1,), (1,)), ((), ())),
                preferred_element_type=F32)
    low = projected[:, :RANK].astype(BF16)
    for n in range(NSTATE):
        for ref, at in ((b_ref, RANK), (c_ref, RANK + NSTATE)):
            column = projected[:, at + n : at + n + 1]
            ref[pl.ds(n, ROWS, stride=NSTATE), :] = jnp.broadcast_to(column, (ROWS, 128))

    for kx in range(NX):
        for ky in range(NY):
            rhs = jnp.concatenate([wdt[kc * NX + kx][ky] for kc in range(NC)], 1)
            both = jnp.dot(low, rhs, preferred_element_type=F32)
            for kc, q in enumerate(place(ky, kx)):
                dt = softplus(both[:, kc * 128 : (kc + 1) * 128] + bias_ref[:, tile_of(q)])
                g, s = q // 8, q % 8
                dt_ref[g, pl.ds(s, ROWS, stride=8), :] = dt
                dtx_ref[g, pl.ds(s, ROWS, stride=8), :] = dt * inner_ref[:, tile_of(q)]

    def group(g, carry):
        a = [a_ref[pl.ds(pl.multiple_of(g * 128 + n * 8, 8), 8), :] for n in range(NSTATE)]

        def advance(t, hs):
            at = pl.ds(pl.multiple_of(t * 8, 8), 8)
            dt, dtx = dt_ref[g, at, :], dtx_ref[g, at, :]
            new = [
                jnp.exp2(dt * a[n]) * hs[n] + dtx * b_ref[pl.ds(t * NSTATE + n, 1), :]
                for n in range(NSTATE)
            ]
            return (*new, hs[NSTATE] + dt)

        hs = lax.fori_loop(
            0, ROWS, advance, tuple(jnp.zeros((8, 128), F32) for _ in range(NSTATE + 1)), unroll=16
        )
        for n in range(NSTATE):
            state[pl.ds(pl.multiple_of(g * 128 + n * 8, 8), 8), :] = hs[n]
        steps[pl.ds(pl.multiple_of(g * 8, 8), 8), :] = hs[NSTATE]
        return carry

    lax.fori_loop(0, GROUPS, group, 0)
    for h in range(2):
        pack(
            payload_ref.at[h], state[h * HALF : (h + 1) * HALF, :],
            steps[h * STEPPED : (h + 1) * STEPPED, :])


def pack(ref, state, steps):
    ref[:HALF, :] = state.astype(BF16)
    high = steps.astype(BF16)
    ref[HALF : HALF + STEPPED, :] = high
    ref[HALF + STEPPED :, :] = (steps - high.astype(F32)).astype(BF16)


def unpack(ref):
    value = ref[...].astype(F32)
    return value[:HALF], value[HALF : HALF + STEPPED] + value[HALF + STEPPED :]


def half_of(a_ref, h):
    return a_ref[pl.ds(pl.multiple_of(h * HALF, 16), HALF), :]


def chain(a, earlier, later):
    s = later[1].reshape(GROUPS // 2, 1, 8, 128)
    factor = jnp.exp2(a.reshape(GROUPS // 2, NSTATE, 8, 128) * s).reshape(HALF, 128)
    return factor * earlier[0] + later[0], earlier[1] + later[1]


def chip_kernel(place_ref, a_ref, own_ref, other_ref, payload_ref):
    core = place_ref[2]
    own, other = unpack(own_ref.at[core]), unpack(other_ref.at[core])
    first = tuple(jnp.where(core == 1, b, a) for a, b in zip(own, other))
    second = tuple(jnp.where(core == 1, a, b) for a, b in zip(own, other))
    pack(payload_ref, *chain(half_of(a_ref, core), first, second))


def prefix(a, stack, refs, place, total):
    count = len(refs)
    for k, ref in enumerate(refs):
        stack[k] = ref[...]

    def hop(i, carry):
        mine, run = carry
        block = unpack(stack.at[lax.rem(place - i + count, count)])
        new = chain(a, run, block)
        before = i < place
        mine = tuple(jnp.where(before, u, v) for u, v in zip(new, mine))
        return mine, new

    zero = (jnp.zeros((HALF, 128), F32), jnp.zeros((STEPPED, 128), F32))
    return lax.fori_loop(0, count if total else place, hop, (zero, zero))


def row_kernel(place_ref, a_ref, *refs):
    blocks, (payload_ref, state_ref, steps_ref, stack) = refs[:NX], refs[NX:]
    mine, run = prefix(half_of(a_ref, place_ref[2]), stack, blocks, place_ref[1], True)
    pack(payload_ref, *run)
    state_ref[...], steps_ref[...] = mine


def ahead_kernel(place_ref, a_ref, *refs):
    blocks, (state_ref, steps_ref, ahead_ref, stack) = refs[:NY], refs[NY:]
    a = half_of(a_ref, place_ref[2])
    _, run = prefix(a, stack, blocks, place_ref[0], False)
    run = chain(a, run, (state_ref[...], steps_ref[...]))
    ahead_ref[...] = run[0].astype(BF16)


def scan_kernel(place_ref, a_ref, *refs):
    (ahead_ref, other_ahead_ref, other_ref,
     dt_ref, dtx_ref, b_ref, c_ref, inner_ref, x_ref, skip_ref, gain_ref, router_ref, ids_ref,
     mixed_ref, halo_ref, sectioned_ref, state, out, moe) = refs
    core = place_ref[2]
    own = ahead_ref[...].astype(F32)
    swapped = other_ahead_ref[...].astype(F32)
    for h in range(2):
        entering = jnp.where(core == h, own, swapped)
        block = unpack(other_ref.at[h])
        after = chain(a_ref[h * HALF : (h + 1) * HALF, :], (entering, block[1]), block)[0]
        state[h * HALF : (h + 1) * HALF, :] = jnp.where(core == 1, after, entering)

    def group(g, carry):
        a = [a_ref[pl.ds(pl.multiple_of(g * 128 + n * 8, 8), 8), :] for n in range(NSTATE)]

        def advance(t, hs):
            at = pl.ds(pl.multiple_of(t * 8, 8), 8)
            dt, dtx = dt_ref[g, at, :], dtx_ref[g, at, :]
            new, parts = [], []
            for n in range(NSTATE):
                row = pl.ds(t * NSTATE + n, 1)
                h = jnp.exp2(dt * a[n]) * hs[n] + dtx * b_ref[row, :]
                new.append(h)
                part = h * c_ref[row, :]
                if n < 4:
                    parts.append(part)
                else:
                    parts[n % 4] = parts[n % 4] + part
            out[g, at, :] = (parts[0] + parts[1]) + (parts[2] + parts[3])
            return tuple(new)

        start = tuple(
            state[pl.ds(pl.multiple_of(g * 128 + n * 8, 8), 8), :] for n in range(NSTATE)
        )
        lax.fori_loop(0, ROWS, advance, start, unroll=16)
        return carry

    lax.fori_loop(0, GROUPS, group, 0)

    total = jnp.zeros((ROWS, 128), F32)
    for j in range(TILES):
        cols = slice(j * 128, (j + 1) * 128)
        scanned = out[j // 8, pl.ds(j % 8, ROWS, stride=8), :]
        mixed = (
            x_ref[:, cols].astype(F32) + (scanned + skip_ref[:, cols] * inner_ref[:, cols])
        ).astype(BF16)
        mixed_ref[:, cols] = mixed
        halo_ref[:, cols] = mixed[ROWS - HALO :]
        mixed = mixed.astype(F32)
        total = total + mixed * mixed
    scale = lax.rsqrt(jnp.sum(total, axis=1, keepdims=True) * (1.0 / WIDTH) + 1e-06)
    for j in range(TILES // 2):
        cols = slice(j * 256, (j + 1) * 256)
        moe[:, cols] = (mixed_ref[:, cols].astype(F32) * scale * gain_ref[:, cols]).astype(BF16)
    logits = lax.dot_general(
        router_ref[...], moe[...], (((1,), (1,)), ((), ())), preferred_element_type=F32
    )
    one, two = ids_ref[0:1, :], ids_ref[1:2, :]
    expert = lax.broadcasted_iota(jnp.int32, (16, ROWS), 0)
    first = jnp.sum(jnp.where(expert == one, logits, 0.0), axis=0, keepdims=True)
    second = jnp.sum(jnp.where(expert == two, logits, 0.0), axis=0, keepdims=True)
    weight_one = jax.nn.sigmoid(first - second)
    weight = jnp.where(one == 0, weight_one, jnp.where(two == 0, 1.0 - weight_one, 0.0))
    routed = jnp.where((one == 0) | (two == 0), 1.0, 0.0)
    earlier = lax.broadcasted_iota(jnp.int32, (ROWS, ROWS), 0) < lax.broadcasted_iota(
        jnp.int32, (ROWS, ROWS), 1
    )
    ahead_of = jnp.dot(
        jnp.broadcast_to(routed, (8, ROWS)), jnp.where(earlier, 1.0, 0.0), preferred_element_type=F32
    )
    slot = lax.broadcasted_iota(jnp.int32, (SLOTS, ROWS), 0).astype(F32)
    chosen = jnp.where((ahead_of == slot) & (routed > 0.0), 1.0, 0.0)
    weights = chosen * weight
    high = weights.astype(BF16).astype(F32)
    slots = jnp.concatenate([high, weights - high], 0).astype(BF16)
    mixed_ref[:16, WIDTH:] = slots
    mixed_ref[16:, WIDTH:] = jnp.zeros((ROWS - 16, EXTRA), BF16)
    halo_ref[:, WIDTH:] = slots
    sectioned_ref[...] = jnp.dot(
        chosen.astype(BF16), moe[...], preferred_element_type=F32
    ).astype(BF16)


def final_kernel(x_ref, out_ref, y_ref):
    slots = x_ref[:16, WIDTH:]
    for j in range(WIDTH // 512):
        cols = slice(j * 512, (j + 1) * 512)
        y_ref[:, cols] = (x_ref[:, cols].astype(F32) + slot_rows(slots, out_ref, cols)).astype(BF16)


def expert_kernel(*refs):
    pieces, refs = refs[: NC * NY], refs[NC * NY :]
    gate_ref, up_ref, down_ref, own_ref, other_ref, xs = refs
    rows = NX * SLOTS
    for k, piece in enumerate(pieces):
        xs[k * rows : (k + 1) * rows, :] = piece[...]
    gate = jnp.dot(xs[...], gate_ref[...], preferred_element_type=F32)
    up = jnp.dot(xs[...], up_ref[...], preferred_element_type=F32)
    hidden = (gate * jax.nn.sigmoid(gate) * up).astype(BF16)
    half = NY * rows
    for j in range(WIDTH // 512):
        cols = slice(j * 512, (j + 1) * 512)
        terms = jnp.dot(hidden, down_ref[:, cols], preferred_element_type=F32).astype(BF16)
        own_ref[:, cols] = terms[:half]
        other_ref[:, cols] = terms[half:]


def sum_kernel(count, *refs):
    ins, outs = refs[:count], refs[count:]
    rows = outs[0].shape[0]
    for j in range(WIDTH // 512):
        cols = slice(j * 512, (j + 1) * 512)
        total = ins[0][:, cols].astype(F32)
        for ref in ins[1:]:
            total = total + ref[:, cols].astype(F32)
        for k, ref in enumerate(outs):
            ref[:, cols] = total[k * rows : (k + 1) * rows].astype(BF16)


def index(y, x, c):
    return (y % NY) * NX * NC + (x % NX) * NC + c % NC


def shifted(block, dy, dx, dc):
    route = [
        (index(y, x, c), index(y + dy, x + dx, c + dc))
        for y in range(NY)
        for x in range(NX)
        for c in range(NC)
    ]
    return lax.ppermute(block, "seq", route)


def onward(block, sections, distance):
    route = [
        (s * NQ + q, (s + 1) % sections * NQ + q + distance)
        for s in range(sections)
        for q in range(NQ)
        if q + distance < NQ
    ]
    return lax.ppermute(block, ("section", "seq"), route)


def crossed(block, first, second):
    route = []
    for y in range(NY):
        for x in range(NX):
            route.append((index(y, x, 0), index(y + second, x + first, 0)))
            route.append((index(y, x, 1), index(y + first, x + second, 1)))
    return lax.ppermute(block, "seq", route)


def along_x(block):
    return [block] + [shifted(block, 0, k, 0) for k in range(1, NX)]


def along_y(block):
    return [block] + [shifted(block, k, 0, 0) for k in range(1, NY)]


def along_core(blocks):
    return list(blocks) + [shifted(block, 0, 0, 1) for block in blocks]


def body(
    input_in_transit,
    mixer_norm_gain,
    convolution_weight,
    convolution_bias,
    input_projection,
    step_size_projection,
    step_size_bias,
    log_decay_rates,
    mixer_skip_weight,
    expert_norm_gain,
    router,
    gate_weight,
    up_weight,
    down_weight,
    expert_index_table,
):
    sections = lax.axis_size("section")
    q = lax.axis_index("seq")
    y, x, c = q // (NX * NC), q // NC % NX, q % NC
    place = jnp.stack([y, x, c]).astype(jnp.int32)
    sds = jax.ShapeDtypeStruct

    rates = (-LOG2E) * jnp.exp(log_decay_rates[0])
    rates = rates.reshape(GROUPS, 8, 128, NSTATE).transpose(0, 3, 1, 2)
    rates = rates.reshape(GROUPS * NSTATE * 8, 128)
    router_t = router[0].T
    ids = expert_index_table[:, 0].transpose(0, 2, 1)

    kc, ky, kx = jnp.meshgrid(jnp.arange(NC), jnp.arange(NY), jnp.arange(NX), indexing="ij")
    order = (y - ky) % NY * (NX * NC) + (x - kx) % NX * NC + (c + kc) % NC
    order = order.reshape(NQ).astype(jnp.int32)

    present = input_in_transit[0]
    behind = lax.ppermute(present[ROWS - HALO :], "seq", [(i, i + 1) for i in range(NQ - 1)])
    gains = [mixer_norm_gain, convolution_weight[0], convolution_bias]
    inner_shape = sds((ROWS, WIDTH), F32)
    rows = pltpu.VMEM((HALO + ROWS, WIDTH), F32)

    w = jnp.stack(along_x(input_projection[0].T))
    wdt = jnp.stack(along_y(step_size_projection[0]))
    (inner,) = call(
        functools.partial(pre_kernel, True), [present, behind, *gains], [inner_shape], [rows], name="pre"
    )
    w, wdt, inner, rates, order, place, router_t, ids = lax.optimization_barrier(
        (w, wdt, inner, rates, order, place, router_t, ids)
    )
    w, wdt = along_core(along_y(w)), along_core(along_x(wdt))

    handed = None
    for step in range(STEPS):
        if step:
            inner, present = call(
                functools.partial(pre_kernel, False), [*handed, *gains],
                [inner_shape, sds((ROWS, WIDTH), BF16)], [rows], name="pre_next")
        wide = sds((GROUPS, ROWS * 8, 128), F32)
        tall = sds((ROWS * NSTATE, 128), F32)
        packed = sds((PAYLOAD, 128), BF16)
        halves = sds((2, PAYLOAD, 128), BF16)
        states = pltpu.VMEM((GROUPS * NSTATE * 8, 128), F32)
        stack = pltpu.VMEM((NX, PAYLOAD, 128), BF16)
        dt, dtx, b, c_out, payload = call(
            main_kernel, [order, inner, step_size_bias, rates, *w, *wdt],
            [wide, wide, tall, tall, halves], [states, pltpu.VMEM((TILES, 128), F32)], n_smem=1,
            name="project_and_end", mib=24)
        other = shifted(payload, 0, 0, 1)
        (chip,) = call(chip_kernel, [place, rates, payload, other], [packed], n_smem=1, name="chip", mib=8)
        chips, row_state, row_steps = call(
            row_kernel, [place, rates, *along_x(chip)],
            [packed, sds((HALF, 128), F32), sds((STEPPED, 128), F32)], [stack], n_smem=1,
            name="row", mib=8)
        (ahead,) = call(
            ahead_kernel, [place, rates, *along_y(chips), row_state, row_steps],
            [sds((HALF, 128), BF16)], [stack], n_smem=1, name="ahead", mib=8)
        mixed, halo, sectioned = call(
            scan_kernel,
            [place, rates, ahead, shifted(ahead, 0, 0, 1), other, dt, dtx, b, c_out, inner, present,
             mixer_skip_weight, expert_norm_gain, router_t, ids[step]],
            [sds((ROWS, WIDTH + EXTRA), BF16), sds((HALO, WIDTH + EXTRA), BF16), sds((SLOTS, WIDTH), BF16)],
            [states, pltpu.VMEM((GROUPS, ROWS * 8, 128), F32), pltpu.VMEM((ROWS, WIDTH), BF16)],
            n_smem=1, name="scan", mib=24)
        last = step + 1 == STEPS
        if not last:
            handed = [onward(mixed, sections, 0), onward(halo, sections, 1)]
        gathered = [sectioned] + [crossed(sectioned, k, 0) for k in range(1, NX)]
        gathered = jnp.concatenate(gathered, 0)
        gathered = [gathered] + [crossed(gathered, 0, k) for k in range(1, NY)]
        gathered = along_core(gathered)
        half = sds((ROWS, WIDTH), BF16)
        own, others = call(
            expert_kernel, [*gathered, gate_weight[0], up_weight[0], down_weight[0]], [half, half],
            [pltpu.VMEM((NQ * SLOTS, WIDTH), BF16)], name="expert", mib=32)
        own = call(
            functools.partial(sum_kernel, NC), [own, shifted(others, 0, 0, 1)],
            [sds((NX * SLOTS, WIDTH), BF16)] * NY, name="sum_core", mib=8)
        own = call(
            functools.partial(sum_kernel, NY), [own[0]] + [crossed(own[k], 0, -k) for k in range(1, NY)],
            [sds((SLOTS, WIDTH), BF16)] * NX, name="sum_second", mib=8)
        (expert_out,) = call(
            functools.partial(sum_kernel, NX), [own[0]] + [crossed(own[k], -k, 0) for k in range(1, NX)],
            [sds((SLOTS, WIDTH), BF16)], name="sum_first", mib=8)
        if last:
            (produced,) = call(
                final_kernel, [mixed, expert_out], [sds((ROWS, WIDTH), BF16)], name="final", mib=8
            )
        else:
            handed += [onward(expert_out, sections, 0), onward(expert_out, sections, 1)]
    return produced[None]


def solution(mesh):
    return jax.shard_map(
        body,
        mesh=mesh,
        in_specs=(
            P("section", "seq", None),
            P("section", None),
            P("section", None, None),
            P("section", None),
            P("section", "seq", None),
            P("section", None, "seq"),
            P("section", None),
            P("section", None, None),
            P("section", None),
            P("section", None),
            P("section", None, None),
            P("section", None, "seq"),
            P("section", None, "seq"),
            P("section", "seq", None),
            P(None, "section", "seq", None),
        ),
        out_specs=P("section", "seq", None),
        check_vma=False,
    )
```
